32 devices in a mesh: row: 8 (over z, x), col: 4 (over y, core).
Axes of the slice: x: 2, y: 2, z: 4, core: 2. Of those that a mesh axis runs over, the one named last changes fastest.
Arguments:
- incident: float32 [2, 36, 8192], P(None, None, 'row'), may hold values from -24 to 24
- diagonal: float32 [8192], P('row'), may hold values from 1 to 2
- near_blocks: bfloat16 [8, 8, 2, 1024, 1024], P('row', None, None, None, 'col'), may hold values from -0.046875 to 0.046875
- left_factors: bfloat16 [8, 8, 2, 64, 1024], P('row', 'col'), may hold values from -0.0390625 to 0.0390625
- right_factors: bfloat16 [8, 8, 2, 64, 1024], P('row', 'col'), may hold values from -0.1875 to 0.1875
- flags: int32 [8, 8], P('row'), may hold values from 0 to 1, as said below
- ranks: int32 [8, 8], P('row', 'col'), may hold values from 4 to 64
- harmonics: float32 [2, 36, 8192], P(None, None, 'row'), may hold values from -0.0625 to 0.0625
Outputs:
- solution: float32 [2, 36, 8192], P(None, None, 'row')
- coefficients: float32 [2, 36, 36], replicated
The draws below stay inside these ranges and needn't reach their ends.
Inputs may be any that keep to these rules, and one draw needn't show every extreme that they name: `flags`: slot 8 / 2 (the pair of a cluster with itself) is always 1; the ones of a row form one run of slots around it.
All inputs are finite; a program needn't handle non-finite values.
Results may differ from the reference program's by a relative error of at most 0.0013.
Values may be sent and summed in bfloat16 or wider, within the bound.
No kernel may reach another device: no remote copies, remote signals or barrier semaphores. Data moves between devices by JAX's collectives and lax.ppermute only.
A program may use at most 128 MiB of HBM per device.

```python
import math
import jax
import jax.numpy as jnp
from jax import lax

ELEM = 1024
FIELDS = 36
HARM = 36
RMAX = 64
NEAR = 8
NCLUS = 8
NELEM = 8192


def draw_incident(key, part):
    cluster = (jnp.arange(NELEM) // ELEM).astype(jnp.float32)
    amplitude = 0.6 * jnp.power(3.0, cluster / (NCLUS - 1.0))
    values = jax.random.normal(key, (2, FIELDS, NELEM), jnp.float32)
    return jnp.clip(values, -6.0, 6.0) * amplitude[None, None, :]


def draw_flags(key, part):
    half_band = NEAR // 2
    lower_key, upper_key = jax.random.split(key)
    rows = jnp.arange(NCLUS)[:, None]
    lower = jax.random.randint(lower_key, (NCLUS, 1), 0, half_band + 1)
    upper = jax.random.randint(upper_key, (NCLUS, 1), 0, NEAR - half_band)
    lower = jnp.where(rows == 0, half_band, lower)
    upper = jnp.where(rows == 0, NEAR - half_band - 1, upper)
    lower = jnp.where(rows == NCLUS // 2, 0, lower)
    upper = jnp.where(rows == NCLUS // 2, 0, upper)
    offsets = jnp.arange(NEAR)[None, :] - half_band
    return ((offsets >= -lower) & (offsets <= upper)).astype(jnp.int32)


def draw_ranks(key, part):
    values = jax.random.randint(key, (NCLUS, NCLUS), 4, RMAX + 1)
    rows = jnp.arange(NCLUS)[:, None]
    columns = jnp.arange(NCLUS)[None, :]
    values = jnp.where((rows == NCLUS // 2) & (columns == 0), RMAX, values)
    values = jnp.where((rows == NCLUS // 2) & (columns == NCLUS - 1), 4, values)
    return values.astype(jnp.int32)


def levels(own_key, shape, shards, smallest, top_value):
    def one(dim, parts):
        steps = jax.random.uniform(jax.random.fold_in(jax.random.fold_in(own_key, 6), dim), (parts,), jnp.float32, smallest / len(shards), top_value / len(shards))
        return jnp.repeat(jnp.exp(steps), shape[dim] // parts).reshape((-1,) + (1,) * (len(shape) - dim - 1))

    gain = one(*shards[0])
    for cut in shards[1:]:
        gain = gain * one(*cut)
    return gain


def gaussian(stream_key, dims, deviation, limit, cuts=(), held_as=jnp.bfloat16):
    level = levels(stream_key, dims, cuts, -0.22, 0.18) if cuts else 1.0
    values = jax.random.normal(stream_key, dims, jnp.float32) * deviation * level
    return jnp.minimum(jnp.maximum(values, -limit), limit).astype(held_as)


def setup_inputs(seed: int = 0) -> dict:
    seeds = jax.random.split(jax.random.key(seed), 9)
    return {
        "incident": draw_incident(jax.random.fold_in(seeds[8], 71), 0),
        "diagonal": jnp.clip(jnp.exp(math.log(2.0) - 0.6931472 * jax.random.uniform(seeds[1], (NELEM,), jnp.float32) ** levels(seeds[1], (NELEM,), ((0, 8),), -0.2, 0.2)), 1.0, 2.0),
        "near_blocks": gaussian(seeds[2], (NCLUS, NEAR, 2, ELEM, ELEM), (16 * ELEM) ** -0.5, 0.046875, ((0, 8), (4, 4))),
        "left_factors": gaussian(seeds[3], (NCLUS, NCLUS, 2, RMAX, ELEM), (384 * RMAX) ** -0.5, 0.0390625, ((0, 8), (1, 4))),
        "right_factors": gaussian(seeds[4], (NCLUS, NCLUS, 2, RMAX, ELEM), ELEM ** -0.5, 0.1875, ((0, 8), (1, 4))),
        "flags": draw_flags(jax.random.fold_in(seeds[8], 71), 0),
        "ranks": draw_ranks(jax.random.fold_in(seeds[8], 71), 0),
        "harmonics": gaussian(seeds[7], (2, HARM, NELEM), NELEM ** -0.5, 0.0625, ((2, 8),), jnp.float32),
    }


highest = lax.Precision.HIGHEST

def dense_term(vector, block):

    def product(left, right):
        return jnp.einsum('sf,ef->se', left, right, precision=highest)
    real_out = product(vector[0], block[0]) - product(vector[1], block[1])
    imag_out = product(vector[0], block[1]) + product(vector[1], block[0])
    return jnp.stack([real_out, imag_out])

def lowrank_term(vector, left_block, right_block, rank):

    def inner(left, right):
        return jnp.einsum('sf,rf->sr', left, right, precision=highest)

    def outer(left, right):
        return jnp.einsum('sr,re->se', left, right, precision=highest)
    coeff_real = inner(vector[0], right_block[0]) - inner(vector[1], right_block[1])
    coeff_imag = inner(vector[0], right_block[1]) + inner(vector[1], right_block[0])
    keep = (jnp.arange(right_block.shape[1], dtype=jnp.int32) < rank)[None, None, :]
    coeffs = jnp.where(keep, jnp.stack([coeff_real, coeff_imag]), 0.0)
    coeffs = lax.optimization_barrier(coeffs.astype(jnp.bfloat16)).astype(jnp.float32)
    real_out = outer(coeffs[0], left_block[0]) - outer(coeffs[1], left_block[1])
    imag_out = outer(coeffs[0], left_block[1]) + outer(coeffs[1], left_block[0])
    return jnp.stack([real_out, imag_out])

def apply_operator(vector, diagonal, near_blocks, left_factors, right_factors, flags, ranks):
    rounded = lax.optimization_barrier(vector.astype(jnp.bfloat16)).astype(jnp.float32)
    pieces = rounded.reshape(2, FIELDS, NCLUS, ELEM).transpose(2, 0, 1, 3)
    half_band = NEAR // 2

    def one_row(row_index):

        def add_near(total, slot):
            target = (row_index + slot - half_band) % NCLUS
            term = lax.cond(flags[row_index, slot] == 1, lambda operand: dense_term(operand, near_blocks[row_index, slot].astype(jnp.float32)), lambda operand: jnp.zeros((2, FIELDS, ELEM), jnp.float32), pieces[target])
            return (total + term, None)

        def add_far(total, column_index):
            offset = (column_index - row_index + half_band) % NCLUS
            is_near = (offset < NEAR) & (flags[row_index, jnp.minimum(offset, NEAR - 1)] == 1)
            term = lax.cond(is_near, lambda operand: jnp.zeros((2, FIELDS, ELEM), jnp.float32), lambda operand: lowrank_term(operand, left_factors[row_index, column_index].astype(jnp.float32), right_factors[row_index, column_index].astype(jnp.float32), ranks[row_index, column_index]), pieces[column_index])
            return (total + term, None)
        total, _ = lax.scan(add_near, jnp.zeros((2, FIELDS, ELEM), jnp.float32), jnp.arange(NEAR, dtype=jnp.int32))
        total, _ = lax.scan(add_far, total, jnp.arange(NCLUS, dtype=jnp.int32))
        return total
    rows = lax.map(one_row, jnp.arange(NCLUS, dtype=jnp.int32))
    products = rows.transpose(1, 2, 0, 3).reshape(2, FIELDS, NELEM)
    return products + diagonal[None, None, :] * vector

def inner_products(first, second):
    return jnp.einsum('csn,ctn->st', first, second, precision=highest)

def combine_rows(matrix, vectors):
    return jnp.einsum('st,ctn->csn', matrix, vectors, precision=highest)

def matmul(left, right):
    return jnp.dot(left, right, precision=highest)

def lower_inverse(lower):
    identity = jnp.eye(lower.shape[0], dtype=lower.dtype)
    return lax.linalg.triangular_solve(lower, identity, left_side=True, lower=True)

def project(harmonics, vectors):

    def contract(left, right):
        return jnp.einsum('mn,sn->ms', left, right, precision=highest)
    real_out = contract(harmonics[0], vectors[0]) + contract(harmonics[1], vectors[1])
    imag_out = contract(harmonics[0], vectors[1]) - contract(harmonics[1], vectors[0])
    return jnp.stack([real_out, imag_out])

def reference(incident, diagonal, near_blocks, left_factors, right_factors, flags, ranks, harmonics):

    def operator(vector):
        return apply_operator(vector, diagonal, near_blocks, left_factors, right_factors, flags, ranks)
    lower_first = jnp.linalg.cholesky(inner_products(incident, incident))
    basis_one = combine_rows(lower_inverse(lower_first), incident)
    image = operator(basis_one)
    coupling_one = inner_products(image, basis_one)
    rest = image - combine_rows(coupling_one, basis_one)
    gram_one = inner_products(rest, rest)
    lower_second = jnp.linalg.cholesky(gram_one)
    basis_two = combine_rows(lower_inverse(lower_second), rest)
    image = operator(basis_two)
    coupling_onetwo = inner_products(image, basis_one)
    coupling_two = inner_products(image, basis_two)
    rest = image - combine_rows(coupling_onetwo, basis_one) - combine_rows(coupling_two, basis_two)
    gram_two = inner_products(rest, rest)
    upper_left = matmul(coupling_one, coupling_one.T) + gram_one
    upper_right = matmul(coupling_one, coupling_onetwo.T) + matmul(lower_second, coupling_two.T)
    lower_right = matmul(coupling_onetwo, coupling_onetwo.T) + matmul(coupling_two, coupling_two.T) + gram_two
    normal = jnp.concatenate([jnp.concatenate([upper_left, upper_right], axis=1), jnp.concatenate([upper_right.T, lower_right], axis=1)], axis=0)
    target = jnp.concatenate([matmul(lower_first, coupling_one.T), matmul(lower_first, coupling_onetwo.T)], axis=1)
    factor_inverse = lower_inverse(jnp.linalg.cholesky(normal))
    weights = matmul(factor_inverse.T, matmul(factor_inverse, target.T)).T
    solution = combine_rows(weights[:, :FIELDS], basis_one) + combine_rows(weights[:, FIELDS:], basis_two)
    return (solution, project(harmonics, solution))
```

```python
import functools

import jax
import jax.numpy as jnp
from jax import lax
from jax.experimental import pallas as pl
from jax.experimental.pallas import tpu as pltpu
from jax.sharding import PartitionSpec as P

F32 = jnp.float32
BF16 = jnp.bfloat16
SHIFT = 1.5
highest = lax.Precision.HIGHEST
VMEM = pltpu.CompilerParams(vmem_limit_bytes=40 * 1024 * 1024)


def dot_t(left, right, precision=None):
    return lax.dot_general(
        left, right, (((1,), (1,)), ((), ())), precision=precision, preferred_element_type=F32
    )


def dot_n(left, right, precision=highest):
    return lax.dot_general(
        left, right, (((1,), (0,)), ((), ())), precision=precision, preferred_element_type=F32
    )


def xor(a, b):
    bit = 1
    while bit <= b:
        if b & bit:
            a = a + bit - 2 * bit * ((a // bit) % 2)
        bit *= 2
    return a


def near_kernel(rows, slots, pos, v_ref, block_ref, out_ref, first, second):
    k = pl.program_id(0)
    cols, both, width = out_ref.shape
    half = both // 2

    @pl.when(k == 0)
    def _():
        first[...] = jnp.zeros_like(first)
        second[...] = jnp.zeros_like(second)

    @pl.when(pos[2 + k] == 1)
    def _():
        v = v_ref[(pos[0] + k - slots // 2 + rows) % rows]
        first[...] += dot_t(v, block_ref[0, 0, 0])
        second[...] += dot_t(v, block_ref[0, 0, 1])

    @pl.when(k == slots - 1)
    def _():
        for q in range(cols):
            part = pl.ds(q * width, width)
            place = jnp.bitwise_xor(pos[1], q)
            out_ref[place, :half] = first[:half, part] - second[half:, part]
            out_ref[place, half:] = first[half:, part] + second[:half, part]


def near(pos, v, blocks, cols):
    rows, both, width = v.shape
    _, slots, _, elements, _ = blocks.shape

    def which(k, pos):
        lo = slots
        hi = 0
        for s in reversed(range(slots)):
            lo = jnp.where(pos[2 + s] == 1, s, lo)
        for s in range(slots):
            hi = jnp.where(pos[2 + s] == 1, s, hi)
        return (0, jnp.clip(k, jnp.minimum(lo, hi), hi), 0, 0, 0)

    return pl.pallas_call(
        functools.partial(near_kernel, rows, slots),
        grid_spec=pltpu.PrefetchScalarGridSpec(
            num_scalar_prefetch=1,
            grid=(slots,),
            in_specs=[
                pl.BlockSpec((rows, both, width), lambda k, pos: (0, 0, 0)),
                pl.BlockSpec((1, 1, 2, elements, width), which),
            ],
            out_specs=pl.BlockSpec((cols, both, width), lambda k, pos: (0, 0, 0)),
            scratch_shapes=[
                pltpu.VMEM((both, elements), F32),
                pltpu.VMEM((both, elements), F32),
            ],
        ),
        out_shape=jax.ShapeDtypeStruct((cols, both, width), F32),
        compiler_params=VMEM,
        name="near",
    )(pos, v, blocks)


def far_kernel(blocks, rank, pos, v_ref, r_ref, l_ref, start_ref, out_ref, total):
    s = pl.program_id(0)
    cols, both, width = out_ref.shape
    half = both // 2
    column = jnp.bitwise_xor(pos[1], s)
    low = lax.broadcasted_iota(jnp.int32, (half, 2 * rank), 1) < rank
    upper, lower = [], []
    for b in range(blocks):
        t = dot_t(v_ref[column * blocks + b], r_ref[0, b].reshape(2 * rank, width))
        turned = pltpu.roll(t, rank, 1)
        z = jnp.where(low, t[:half] - turned[half:], t[:half] + turned[half:])
        upper.append(jnp.where(low, z, -z))
        lower.append(pltpu.roll(z, rank, 1))
    mixed = jnp.concatenate(
        [jnp.concatenate(upper, axis=1), jnp.concatenate(lower, axis=1)], axis=0
    ).astype(BF16)
    left = l_ref[0].reshape(blocks * 2 * rank, l_ref.shape[-1])
    term = lax.dot_general(mixed, left, (((1,), (0,)), ((), ())), preferred_element_type=F32)

    @pl.when(s == 0)
    def _():
        total[...] = term

    @pl.when(s > 0)
    def _():
        total[...] += term

    @pl.when(s == cols - 1)
    def _():
        for q in range(cols):
            place = jnp.bitwise_xor(pos[1], q)
            out_ref[place] = start_ref[place] + total[:, q * width : (q + 1) * width]


def far(pos, v, right, left, start):
    rows, both, width = v.shape
    cols, blocks, _, rank, elements = left.shape
    whole = lambda s, pos: (0, 0, 0)
    mine = lambda s, pos: (s, 0, 0, 0, 0)
    return pl.pallas_call(
        functools.partial(far_kernel, blocks, rank),
        grid_spec=pltpu.PrefetchScalarGridSpec(
            num_scalar_prefetch=1,
            grid=(cols,),
            in_specs=[
                pl.BlockSpec((rows, both, width), whole),
                pl.BlockSpec((1, blocks, 2, rank, width), mine),
                pl.BlockSpec((1, blocks, 2, rank, elements), mine),
                pl.BlockSpec((cols, both, width), whole),
            ],
            out_specs=pl.BlockSpec((cols, both, width), whole),
            scratch_shapes=[pltpu.VMEM((both, elements), F32)],
        ),
        out_shape=jax.ShapeDtypeStruct((cols, both, width), F32),
        compiler_params=VMEM,
        name="far",
    )(pos, v, right, left, start)


def gram_one_kernel(shift, b_ref, p_ref, h_ref, out_ref):
    slots, both, _ = b_ref.shape
    half = both // 2
    grams = jnp.zeros((2 * half, half), F32)
    shots = jnp.zeros((both, 2 * both), F32)
    for s in range(slots):
        b, p, h = b_ref[s], p_ref[s], h_ref[s]
        ab = p + shift * b
        for part in range(2):
            rows = slice(part * half, (part + 1) * half)
            grams += dot_t(jnp.concatenate([ab[rows], b[rows]], axis=0), ab[rows], highest)
        shots += dot_t(h, jnp.concatenate([b, p], axis=0), highest)
    out_ref[0] = grams[:half]
    out_ref[1] = grams[half:]
    for n in range(2):
        q = shots[:, n * both : (n + 1) * both]
        out_ref[2 + 2 * n] = q[:half, :half] + q[half:, half:]
        out_ref[3 + 2 * n] = q[:half, half:] - q[half:, :half]


def gram_two_kernel(shift, b_ref, p_ref, a_ref, out_ref):
    slots, both, _ = b_ref.shape
    half = both // 2
    total = jnp.zeros((half, 3 * half), F32)
    for s in range(slots):
        for part in range(2):
            rows = slice(part * half, (part + 1) * half)
            b, p, a = b_ref[s, rows], p_ref[s, rows], a_ref[s, rows]
            total += dot_t(a, jnp.concatenate([a, p + shift * b, b], axis=0), highest)
    out_ref[...] = total


def eliminate(m, size):
    index = lax.broadcasted_iota(jnp.int32, m.shape, 0)
    for k in range(size):
        row = m[k : k + 1, :] / m[k : k + 1, k : k + 1]
        m = jnp.where(index == k, row, m - m[:, k : k + 1] * row)
    return m


def unit_padding(size, fields):
    r = lax.broadcasted_iota(jnp.int32, (size, size), 0)
    c = lax.broadcasted_iota(jnp.int32, (size, size), 1)
    return jnp.where((r == c) & (r >= fields), 1.0, 0.0)


def invert_kernel(fields, g1_ref, out_ref):
    half = g1_ref.shape[1]
    pad = unit_padding(half, fields)
    r = lax.broadcasted_iota(jnp.int32, (half, half), 0)
    c = lax.broadcasted_iota(jnp.int32, (half, half), 1)
    eye = jnp.where(r == c, 1.0, 0.0)
    m = jnp.concatenate([g1_ref[0] + pad, eye, g1_ref[1].T], axis=1)
    m = eliminate(m, fields)
    out_ref[...] = m[:, half:]


def solve_kernel(fields, pos, inv_ref, g1_ref, g2_ref, b_ref, p_ref, x_ref, c_ref):
    half = inv_ref.shape[0]
    cols, both, width = p_ref.shape
    g2 = g2_ref[0]
    for n in range(1, g2_ref.shape[0]):
        g2 = g2 + g2_ref[n]
    z22 = g2[:, :half] + unit_padding(half, fields)
    z21 = g2[:, half : 2 * half]
    z2b = g2[:, 2 * half : 3 * half]
    inv = inv_ref[:, :half]
    w1b = inv_ref[:, half:]
    step = dot_n(z21, jnp.concatenate([dot_t(inv, z21, highest), w1b], axis=1))
    m = eliminate(jnp.concatenate([z22, z2b], axis=1) - step, fields)
    w2 = m[:, half:]
    w1 = w1b - dot_n(inv, lax.dot_general(z21, w2, (((0,), (0,)), ((), ())), precision=highest, preferred_element_type=F32))
    y1 = w1.T
    y2 = w2.T
    for n in range(2):
        total = dot_t(g1_ref[2 + n], y1, highest) + dot_t(g1_ref[4 + n], y2, highest)
        c_ref[n] = total[:fields, :fields]
    y = jnp.concatenate([y1, y2], axis=1)
    for q in range(cols):
        place = jnp.bitwise_xor(pos[1], q)
        for part in range(2):
            rows = slice(part * half, (part + 1) * half)
            basis = jnp.concatenate([b_ref[place, rows], p_ref[place, rows]], axis=0)
            x = dot_n(y, basis)
            x_ref[part, :, q * width : (q + 1) * width] = x[:fields]


def whole_call(kernel, out_shape, name, *args, scalars=0):
    vmem = pl.BlockSpec(memory_space=pltpu.VMEM)
    smem = pl.BlockSpec(memory_space=pltpu.SMEM)
    single = not isinstance(out_shape, (list, tuple))
    return pl.pallas_call(
        kernel,
        in_specs=[smem] * scalars + [vmem] * (len(args) - scalars),
        out_specs=vmem if single else [vmem] * len(out_shape),
        out_shape=out_shape,
        compiler_params=VMEM,
        name=name,
    )(*args)


def swap(array, axis, bit):
    size = lax.axis_size(axis)
    return lax.ppermute(array, axis, [(n, n ^ bit) for n in range(size)])


def spread(array, axis):
    size = lax.axis_size(axis)
    copies = jnp.broadcast_to(array[None], (size,) + array.shape)
    return lax.all_to_all(copies, axis, 0, 0)


def body(incident, diagonal, near_blocks, left_factors, right_factors, flags, ranks, harmonics):
    _, blocks, _, rank, elements = left_factors.shape
    slots, width = near_blocks.shape[1], near_blocks.shape[4]
    fields = incident.shape[1]
    cols, rows = lax.axis_size("col"), lax.axis_size("row")
    row_index, column = lax.axis_index("row"), lax.axis_index("col")
    half = -(-fields // 8) * 8
    pos = jnp.concatenate([jnp.stack([row_index, column]).astype(jnp.int32), flags[0]])
    bits = [1 << n for n in range(cols.bit_length() - 1)]

    def place(s):
        return jnp.bitwise_xor(column, s) * width

    def cut(array, s):
        piece = lax.dynamic_slice_in_dim(array, place(s), width, 2)
        piece = jnp.pad(piece, ((0, 0), (0, half - array.shape[1]), (0, 0)))
        return piece.reshape(2 * half, width)

    cluster = column * blocks + jnp.arange(blocks, dtype=jnp.int32)
    offset = (cluster - row_index + slots // 2) % rows
    is_near = (offset < slots) & (flags[0][jnp.minimum(offset, slots - 1)] == 1)
    keep = (jnp.arange(rank)[None, :] < ranks[0][:, None]) & ~is_near[:, None]
    masked = jnp.where(keep[:, None, :, None], right_factors[0], jnp.zeros((), BF16))
    rights = {(0, s): lax.dynamic_slice_in_dim(masked, place(s), width, 3) for s in range(cols)}
    lefts = {0: left_factors[0]}
    for bit in reversed(bits):
        keys = [key for key in rights if key[1] & bit]
        arrived = swap(jnp.stack([rights.pop(key) for key in keys]), "col", bit)
        for n, (blk, part) in enumerate(keys):
            rights[blk ^ bit, part ^ bit] = arrived[n]
        keys = list(lefts)
        arrived = swap(jnp.stack([lefts[key] for key in keys]), "col", bit)
        for n, key in enumerate(keys):
            lefts[key ^ bit] = arrived[n]
    right_all = jnp.stack([rights[s, 0] for s in range(cols)])
    left_all = jnp.stack([lefts[s] for s in range(cols)])

    def operator(vector):
        gathered = spread(vector, "row")
        total = near(pos, gathered, near_blocks, cols)
        total = far(pos, gathered, right_all, left_all, total)
        total = total[0::2] + swap(total[1::2], "col", 1)
        for bit in bits[1:]:
            other = swap(total, "col", bit)
            total = total + jnp.stack([other[s ^ (bit // 2)] for s in range(cols // 2)])
        return total

    b_all = jnp.stack([cut(incident, s) for s in range(cols)])
    b_own = b_all[0::2]
    h_own = jnp.stack([cut(harmonics, s) for s in range(0, cols, 2)])
    d_own = jnp.stack(
        [lax.dynamic_slice_in_dim(diagonal, place(s), width, 0) for s in range(0, cols, 2)]
    )[:, None, :] - SHIFT

    p_own = operator(b_all[0].astype(BF16)) + d_own * b_own
    p_other = swap(p_own, "col", 1)
    p_all = jnp.stack([p_own, p_other], axis=1).reshape(cols, 2 * half, width)
    one = whole_call(
        functools.partial(gram_one_kernel, SHIFT),
        jax.ShapeDtypeStruct((6, half, half), F32),
        "gram_one",
        b_own,
        p_own,
        h_own,
    )
    one = one + swap(one, "col", 1)
    one = lax.psum(one, "row")

    ap = operator(p_own[0].astype(BF16)) + (d_own + SHIFT) * p_own
    two = whole_call(
        functools.partial(gram_two_kernel, SHIFT),
        jax.ShapeDtypeStruct((half, 3 * half), F32),
        "gram_two",
        b_own,
        p_own,
        ap,
    )
    two = spread(two + swap(two, "col", 1), "row")
    inverse = whole_call(
        functools.partial(invert_kernel, fields),
        jax.ShapeDtypeStruct((half, 2 * half), F32),
        "invert",
        one,
    )
    return tuple(
        whole_call(
            functools.partial(solve_kernel, fields),
            [
                jax.ShapeDtypeStruct((2, fields, elements), F32),
                jax.ShapeDtypeStruct((2, harmonics.shape[1], fields), F32),
            ],
            "solve",
            pos,
            inverse,
            one,
            two,
            b_all,
            p_all,
            scalars=1,
        )
    )


def solution(mesh):
    in_specs = (
        P(None, None, "row"),
        P("row"),
        P("row", None, None, None, "col"),
        P("row", "col", None, None, None),
        P("row", "col", None, None, None),
        P("row", None),
        P("row", "col"),
        P(None, None, "row"),
    )
    out_specs = (P(None, None, "row"), P())
    return jax.shard_map(body, mesh=mesh, in_specs=in_specs, out_specs=out_specs, check_vma=False)
```

```python
import functools

import jax
import jax.numpy as jnp
from jax import lax
from jax.experimental import pallas as pl
from jax.experimental.pallas import tpu as pltpu
from jax.sharding import PartitionSpec as P

F32 = jnp.float32
BF16 = jnp.bfloat16
SHIFT = 1.5
highest = lax.Precision.HIGHEST
MIB = 1024 * 1024


def dot_t(left, right, precision=None):
    return lax.dot_general(
        left, right, (((1,), (1,)), ((), ())), precision=precision, preferred_element_type=F32
    )


def dot_n(left, right, precision=highest):
    return lax.dot_general(
        left, right, (((1,), (0,)), ((), ())), precision=precision, preferred_element_type=F32
    )


def split(a):
    high = a.astype(BF16)
    return high, (a - high.astype(F32)).astype(BF16)


def dot_split(left, right, dot):
    (lh, ll), (rh, rl) = split(left), split(right)
    return dot(lh, rh, None) + (dot(lh, rl, None) + dot(ll, rh, None))


def cut_kernel(column, r_ref, out_ref):
    cols, _, width = out_ref.shape
    for q in range(cols):
        out_ref[jnp.bitwise_xor(column[0], q)] = r_ref[:, q * width : (q + 1) * width]


def far_in_kernel(blocks, pos, v_ref, r_ref, out_ref):
    places, _, half, both_ranks = out_ref.shape
    rank = both_ranks // 2
    low = lax.broadcasted_iota(jnp.int32, (half, both_ranks), 1) < rank
    for s in range(places):
        column = jnp.bitwise_xor(pos[1], s)
        for b in range(blocks):
            t = dot_t(v_ref[column * blocks + b], r_ref[s, b])
            turned = pltpu.roll(t, rank, 1)
            out_ref[s, b] = jnp.where(low, t[:half] - turned[half:], t[:half] + turned[half:])


def near_kernel(rows, pos, v_ref, blocks_ref, out_ref, held, first, second, sems):
    slots = held.shape[0]
    half = out_ref.shape[0] // 2

    def fetch(k, part):
        return pltpu.make_async_copy(
            blocks_ref.at[0, k, part], held.at[k, part], sems.at[k, part]
        )

    for k in range(slots):
        for part in range(2):
            fetch(k, part).start()
    for k in range(slots):
        v = v_ref[(pos[0] + k - slots // 2 + rows) % rows]
        v = jnp.where(pos[2 + k] == 1, v, jnp.zeros_like(v))
        for part, total in enumerate((first, second)):
            fetch(k, part).wait()
            term = dot_t(v, held[k, part])
            if k == 0:
                total[...] = term
            else:
                total[...] += term
    out_ref[:half] = first[:half] - second[half:]
    out_ref[half:] = first[half:] + second[:half]


def near(pos, v, blocks):
    rows, both, _ = v.shape
    _, slots, _, elements, width = blocks.shape
    return pl.pallas_call(
        functools.partial(near_kernel, rows),
        in_specs=[
            pl.BlockSpec(memory_space=pltpu.SMEM),
            pl.BlockSpec(memory_space=pltpu.VMEM),
            pl.BlockSpec(memory_space=pltpu.HBM),
        ],
        out_specs=pl.BlockSpec(memory_space=pltpu.VMEM),
        out_shape=jax.ShapeDtypeStruct((both, elements), F32),
        scratch_shapes=[
            pltpu.VMEM((slots, 2, elements, width), BF16),
            pltpu.VMEM((both, elements), F32),
            pltpu.VMEM((both, elements), F32),
            pltpu.SemaphoreType.DMA((slots, 2)),
        ],
        compiler_params=pltpu.CompilerParams(vmem_limit_bytes=53 * MIB),
        name="near",
    )(pos, v, blocks)


def far_out_kernel(pos, z_ref, left_ref, near_ref, out_ref):
    places, blocks, half, both_ranks = z_ref.shape
    cols, _, width = out_ref.shape
    rank = both_ranks // 2
    lane = lax.broadcasted_iota(jnp.int32, (half, both_ranks), 1)
    low = lane < rank
    mixed = []
    for s in range(places):
        upper, lower = [], []
        for b in range(blocks):
            used = pos[pos.shape[0] - blocks + b]
            z = jnp.where(lax.rem(lane, rank) < used, z_ref[s, b], 0.0)
            upper.append(jnp.where(low, z, -z))
            lower.append(pltpu.roll(z, rank, 1))
        upper, lower = jnp.concatenate(upper, axis=1), jnp.concatenate(lower, axis=1)
        mixed.append(jnp.concatenate([upper, lower], axis=0).astype(BF16))
    for q in range(cols):
        place = jnp.bitwise_xor(pos[1], q)
        part = slice(q * width, (q + 1) * width)
        term = near_ref[:, part]
        for s in range(places):
            term = term + dot_n(mixed[s], left_ref[s, :, part], None)
        out_ref[place] = term


def gram_one_kernel(shift, b_ref, p_ref, h_ref, out_ref):
    both = b_ref.shape[0]
    half = both // 2
    b, p, h = b_ref[...], p_ref[...], h_ref[...]
    ab = p + shift * b
    grams = jnp.zeros((2 * half, half), F32)
    for part in range(2):
        rows = slice(part * half, (part + 1) * half)
        grams += dot_split(jnp.concatenate([ab[rows], b[rows]], axis=0), ab[rows], dot_t)
    shots = dot_split(h, jnp.concatenate([b, p], axis=0), dot_t)
    pieces = [grams[:half], grams[half:]]
    for n in range(2):
        q = shots[:, n * both : (n + 1) * both]
        pieces.append(q[:half, :half] + q[half:, half:])
        pieces.append(q[:half, half:] - q[half:, :half])
    out_ref[...] = jnp.concatenate(pieces, axis=1)


def gram_two_kernel(shift, pos, b_ref, p_ref, a_ref, out_ref):
    slots, both, _ = b_ref.shape
    half = both // 2
    total = jnp.zeros((half, 3 * half), F32)
    for n in range(slots):
        s = jnp.bitwise_xor(pos[1] // 2, n)
        for part in range(2):
            rows = slice(part * half, (part + 1) * half)
            b, p, a = b_ref[s, rows], p_ref[s, rows], a_ref[s, rows]
            total += dot_split(a, jnp.concatenate([a, p + shift * b, b], axis=0), dot_t)
    out_ref[...] = total


def eliminate(m, size):
    index = lax.broadcasted_iota(jnp.int32, m.shape, 0)
    column = jnp.broadcast_to(m[:, :1], m.shape)
    for k in range(size):
        ahead = jnp.broadcast_to(m[:, k + 1 : k + 2], m.shape)
        scale = 1.0 / column[k : k + 1]
        row = m[k : k + 1] * scale
        first = ahead[k : k + 1] * scale
        m = jnp.where(index == k, row, m - column * row)
        column = jnp.where(index == k, first, ahead - column * first)
    return m


def unit_padding(size, fields):
    r = lax.broadcasted_iota(jnp.int32, (size, size), 0)
    c = lax.broadcasted_iota(jnp.int32, (size, size), 1)
    return jnp.where((r == c) & (r >= fields), 1.0, 0.0)


def invert_kernel(fields, g1_ref, out_ref):
    half = g1_ref.shape[0]
    pad = unit_padding(half, fields)
    r = lax.broadcasted_iota(jnp.int32, (half, half), 0)
    c = lax.broadcasted_iota(jnp.int32, (half, half), 1)
    eye = jnp.where(r == c, 1.0, 0.0)
    m = jnp.concatenate([g1_ref[:, :half] + pad, eye, g1_ref[:, half : 2 * half].T], axis=1)
    m = eliminate(m, fields)
    out_ref[...] = m[:, half:]


def solve_kernel(fields, pos, inv_ref, g1_ref, g2_ref, b_ref, p_ref, x_ref, c_ref):
    half = inv_ref.shape[0]
    cols, both, width = p_ref.shape
    g2 = g2_ref[0]
    for n in range(1, g2_ref.shape[0]):
        g2 = g2 + g2_ref[n]
    z22 = g2[:, :half] + unit_padding(half, fields)
    z21 = g2[:, half : 2 * half]
    z2b = g2[:, 2 * half : 3 * half]
    inv = inv_ref[:, :half]
    w1b = inv_ref[:, half:]
    step = dot_n(z21, jnp.concatenate([dot_t(inv, z21, highest), w1b], axis=1))
    m = eliminate(jnp.concatenate([z22, z2b], axis=1) - step, fields)
    w2 = m[:, half:]
    w1 = w1b - dot_n(inv, lax.dot_general(z21, w2, (((0,), (0,)), ((), ())), precision=highest, preferred_element_type=F32))
    y1 = w1.T
    y2 = w2.T
    for n in range(2):
        hb = g1_ref[:, (2 + n) * half : (3 + n) * half]
        hp = g1_ref[:, (4 + n) * half : (5 + n) * half]
        total = dot_t(hb, y1, highest) + dot_t(hp, y2, highest)
        c_ref[:, n, :] = total[: c_ref.shape[0], :fields]
    y = jnp.concatenate([y1, y2], axis=1)
    for q in range(cols):
        place = jnp.bitwise_xor(pos[1], q)
        for part in range(2):
            rows = slice(part * half, (part + 1) * half)
            basis = jnp.concatenate([b_ref[place, rows], p_ref[place, rows]], axis=0)
            x = dot_split(y, basis, dot_n)
            x_ref[:, part, q * width : (q + 1) * width] = x[:fields]


def whole_call(kernel, out_shape, name, *args, scalars=0, cost=None):
    vmem = pl.BlockSpec(memory_space=pltpu.VMEM)
    smem = pl.BlockSpec(memory_space=pltpu.SMEM)
    single = not isinstance(out_shape, (list, tuple))
    return pl.pallas_call(
        kernel,
        in_specs=[smem] * scalars + [vmem] * (len(args) - scalars),
        out_specs=vmem if single else [vmem] * len(out_shape),
        out_shape=out_shape,
        cost_estimate=cost,
        compiler_params=pltpu.CompilerParams(vmem_limit_bytes=12 * MIB),
        name=name,
    )(*args)


def swap(array, axis, bit):
    size = lax.axis_size(axis)
    return lax.ppermute(array, axis, [(n, n ^ bit) for n in range(size)])


def spread(array, axis):
    size = lax.axis_size(axis)
    copies = jnp.broadcast_to(array[None], (size,) + array.shape)
    return lax.all_to_all(copies, axis, 0, 0)


def spread_start(array, axis):
    size = lax.axis_size(axis)
    return jnp.broadcast_to(array[None], (size,) + array.shape)


def body(incident, diagonal, near_blocks, left_factors, right_factors, flags, ranks, harmonics):
    _, blocks, _, rank, elements = left_factors.shape
    slots, width = near_blocks.shape[1], near_blocks.shape[4]
    fields = incident.shape[1]
    cols, rows = lax.axis_size("col"), lax.axis_size("row")
    row_index, column = lax.axis_index("row"), lax.axis_index("col")
    half = -(-fields // 8) * 8
    cluster = column * blocks + jnp.arange(blocks, dtype=jnp.int32)
    offset = (cluster - row_index + slots // 2) % rows
    is_near = jnp.any(
        (offset[:, None] == jnp.arange(slots)[None, :]) & (flags[0][None, :] == 1), axis=1
    )
    used = jnp.where(is_near, 0, ranks[0])
    pos = jnp.concatenate([jnp.stack([row_index, column]).astype(jnp.int32), flags[0], used])
    bits = [1 << n for n in range(cols.bit_length() - 1)]
    row_bits = [1 << n for n in range(rows.bit_length() - 1)]

    def place(s):
        return jnp.bitwise_xor(column, s) * width

    def cut(array, s):
        piece = lax.dynamic_slice_in_dim(array, place(s), width, 2)
        piece = jnp.pad(piece, ((0, 0), (0, half - array.shape[1]), (0, 0)))
        return piece.reshape(2 * half, width)

    b_first = cut(incident, 0)
    copies = spread_start(b_first.astype(BF16), "row")
    copies, right_in = lax.optimization_barrier((copies, right_factors))
    gathered = lax.all_to_all(copies, "row", 0, 0)

    rights = whole_call(
        cut_kernel,
        jax.ShapeDtypeStruct((cols, blocks * 2 * rank, width), BF16),
        "cut",
        column[None].astype(jnp.int32),
        right_in.reshape(blocks * 2 * rank, elements),
        scalars=1,
        cost=pl.CostEstimate(flops=0, bytes_accessed=32 * MIB, transcendentals=0),
    ).reshape(cols, blocks, 2 * rank, width)
    rights = [rights[0]] + [swap(rights[s], "col", s) for s in range(1, cols)]
    rights, gathered = lax.optimization_barrier((rights, gathered))
    lefts = left_factors.reshape(1, blocks * 2 * rank, elements)
    right_all = jnp.stack(rights)

    def operator(gathered, one=None):
        t = whole_call(
            functools.partial(far_in_kernel, blocks),
            jax.ShapeDtypeStruct((cols, blocks, half, 2 * rank), F32),
            "far_in",
            pos,
            gathered,
            right_all,
            scalars=1,
        )
        for _ in bits:
            t = t[0::2] + swap(t[1::2], "col", cols // t.shape[0])
        total = near(pos, gathered, near_blocks)
        if one is not None:
            total, one = lax.optimization_barrier((total, one + swap(one, "row", row_bits[-1])))
        total = whole_call(
            far_out_kernel,
            jax.ShapeDtypeStruct((cols, 2 * half, width), F32),
            "far_out",
            pos,
            t,
            lefts,
            total,
            scalars=1,
        )
        return total if one is None else (total, one)

    total = operator(gathered)
    total = total[0::2] + swap(total[1::2], "col", 1)
    for bit in reversed(bits[1:]):
        n = total.shape[0] // 2
        total = total[:n] + swap(total[n:], "col", bit)
    d_first = lax.dynamic_slice_in_dim(diagonal, place(0), width, 0)
    p_first = total[0] + (d_first - SHIFT)[None, :] * b_first

    copies = spread_start(p_first.astype(BF16), "row")
    copies, p_early = lax.optimization_barrier((copies, p_first))
    gathered = lax.all_to_all(copies, "row", 0, 0)

    one = whole_call(
        functools.partial(gram_one_kernel, SHIFT),
        jax.ShapeDtypeStruct((half, 6 * half), F32),
        "gram_one",
        b_first,
        p_early,
        cut(harmonics, 0),
    )
    for bit in bits:
        one = one + swap(one, "col", bit)
    b_all = jnp.stack([b_first] + [cut(incident, s) for s in range(1, cols)])
    b_own = b_all[0::2]
    p_own = p_early[None]
    for bit in bits[1:]:
        p_own = jnp.concatenate([p_own, swap(p_own, "col", bit)])
    gathered, one, p_own = lax.optimization_barrier((gathered, one, p_own))
    p_all = jnp.stack([p_own, swap(p_own, "col", 1)], axis=1).reshape(cols, 2 * half, width)

    total, one = operator(gathered, one)
    for bit in reversed(row_bits[1:-1]):
        one = one + swap(one, "row", bit)
    total = (total[0::2] + swap(total[1::2], "col", 1)).astype(BF16)
    for bit in bits[1:]:
        other = swap(total, "col", bit).astype(F32)
        total = total.astype(F32) + jnp.stack([other[s ^ (bit // 2)] for s in range(cols // 2)])
        total = total if bit == bits[-1] else total.astype(BF16)
    d_own = jnp.stack(
        [lax.dynamic_slice_in_dim(diagonal, place(s), width, 0) for s in range(0, cols, 2)]
    )
    ap, one = lax.optimization_barrier((total + d_own[:, None, :] * p_own, one))
    one = one + swap(one, "row", row_bits[0])
    two = whole_call(
        functools.partial(gram_two_kernel, SHIFT),
        jax.ShapeDtypeStruct((half, 3 * half), F32),
        "gram_two",
        pos,
        b_own,
        p_own,
        ap,
        scalars=1,
    )
    two = spread(two + swap(two, "col", 1), "row")
    inverse = whole_call(
        functools.partial(invert_kernel, fields),
        jax.ShapeDtypeStruct((half, 2 * half), F32),
        "invert",
        one,
    )
    return tuple(
        array.transpose(1, 0, 2)
        for array in whole_call(
            functools.partial(solve_kernel, fields),
            [
                jax.ShapeDtypeStruct((fields, 2, elements), F32),
                jax.ShapeDtypeStruct((harmonics.shape[1], 2, fields), F32),
            ],
            "solve",
            pos,
            inverse,
            one,
            two,
            b_all,
            p_all,
            scalars=1,
        )
    )


def solution(mesh):
    in_specs = (
        P(None, None, "row"),
        P("row"),
        P("row", None, None, None, "col"),
        P("row", "col", None, None, None),
        P("row", "col", None, None, None),
        P("row", None),
        P("row", "col"),
        P(None, None, "row"),
    )
    out_specs = (P(None, None, "row"), P())
    return jax.shard_map(body, mesh=mesh, in_specs=in_specs, out_specs=out_specs, check_vma=False)
```

```python
import functools

import jax
import jax.numpy as jnp
from jax import lax
from jax.experimental import pallas as pl
from jax.experimental.pallas import tpu as pltpu
from jax.sharding import PartitionSpec as P

F32 = jnp.float32
BF16 = jnp.bfloat16
SHIFT = 1.5
highest = lax.Precision.HIGHEST
MIB = 1024 * 1024


def dot_t(left, right, precision=None):
    return lax.dot_general(
        left, right, (((1,), (1,)), ((), ())), precision=precision, preferred_element_type=F32
    )


def dot_n(left, right, precision=highest):
    return lax.dot_general(
        left, right, (((1,), (0,)), ((), ())), precision=precision, preferred_element_type=F32
    )


def split(a):
    high = a.astype(BF16)
    return high, (a - high.astype(F32)).astype(BF16)


def dot_split(left, right, dot):
    (lh, ll), (rh, rl) = split(left), split(right)
    return dot(lh, rh, None) + (dot(lh, rl, None) + dot(ll, rh, None))


def cut_kernel(column, r_ref, out_ref):
    cols, _, width = out_ref.shape
    for q in range(cols):
        out_ref[jnp.bitwise_xor(column[0], q)] = r_ref[:, q * width : (q + 1) * width]


def far_in_kernel(blocks, pos, v_ref, r_ref, out_ref):
    places, _, half, both_ranks = out_ref.shape
    fields = v_ref.shape[1] // 2
    rank = both_ranks // 2
    low = lax.broadcasted_iota(jnp.int32, (fields, both_ranks), 1) < rank
    out_ref[...] = jnp.zeros_like(out_ref)
    for s in range(places):
        column = jnp.bitwise_xor(pos[1], s)
        for b in range(blocks):
            t = dot_t(v_ref[column * blocks + b], r_ref[s, b])
            real, turned = t[:fields], pltpu.roll(t, rank, 1)[fields:]
            out_ref[s, b, :fields] = jnp.where(low, real - turned, real + turned)


def near_kernel(rows, pos, v_ref, blocks_ref, out_ref, held, first, second, sems):
    slots = held.shape[0]
    half = out_ref.shape[0] // 2

    def fetch(k, part):
        return pltpu.make_async_copy(
            blocks_ref.at[0, k, part], held.at[k, part], sems.at[k, part]
        )

    for k in range(slots):
        for part in range(2):
            fetch(k, part).start()
    for k in range(slots):
        v = v_ref[(pos[0] + k - slots // 2 + rows) % rows]
        v = jnp.where(pos[2 + k] == 1, v, jnp.zeros_like(v))
        for part in range(2):
            fetch(k, part).wait()
        for part, total in enumerate((first, second)):
            term = dot_t(v, held[k, part])
            if k == 0:
                total[...] = term
            else:
                total[...] += term
    fields = v_ref.shape[1] // 2
    out_ref[...] = jnp.zeros_like(out_ref)
    out_ref[:fields] = first[:fields] - second[fields:]
    out_ref[half : half + fields] = first[fields:] + second[:fields]


def near(pos, v, blocks, both):
    rows, twice, _ = v.shape
    _, slots, _, elements, width = blocks.shape
    return pl.pallas_call(
        functools.partial(near_kernel, rows),
        in_specs=[
            pl.BlockSpec(memory_space=pltpu.SMEM),
            pl.BlockSpec(memory_space=pltpu.VMEM),
            pl.BlockSpec(memory_space=pltpu.HBM),
        ],
        out_specs=pl.BlockSpec(memory_space=pltpu.VMEM),
        out_shape=jax.ShapeDtypeStruct((both, elements), F32),
        scratch_shapes=[
            pltpu.VMEM((slots, 2, elements, width), BF16),
            pltpu.VMEM((twice, elements), F32),
            pltpu.VMEM((twice, elements), F32),
            pltpu.SemaphoreType.DMA((slots, 2)),
        ],
        compiler_params=pltpu.CompilerParams(vmem_limit_bytes=53 * MIB),
        name="near",
    )(pos, v, blocks)


def far_out_kernel(pos, z_ref, left_ref, near_ref, out_ref):
    places, blocks, half, both_ranks = z_ref.shape
    cols, _, width = out_ref.shape
    rank = both_ranks // 2
    lane = lax.broadcasted_iota(jnp.int32, (half, both_ranks), 1)
    low = lane < rank
    mixed = []
    for s in range(places):
        upper, lower = [], []
        for b in range(blocks):
            used = pos[pos.shape[0] - blocks + b]
            z = jnp.where(lax.rem(lane, rank) < used, z_ref[s, b], 0.0)
            upper.append(jnp.where(low, z, -z))
            lower.append(pltpu.roll(z, rank, 1))
        upper, lower = jnp.concatenate(upper, axis=1), jnp.concatenate(lower, axis=1)
        mixed.append(jnp.concatenate([upper, lower], axis=0).astype(BF16))
    for q in range(cols):
        place = jnp.bitwise_xor(pos[1], q)
        part = slice(q * width, (q + 1) * width)
        term = near_ref[:, part]
        for s in range(places):
            term = term + dot_n(mixed[s], left_ref[s, :, part], None)
        out_ref[place] = term


def gram_one_kernel(shift, b_ref, p_ref, h_ref, out_ref):
    both = b_ref.shape[0]
    half = both // 2
    b, p, h = b_ref[...], p_ref[...], h_ref[...]
    ab = p + shift * b
    grams = jnp.zeros((2 * half, half), F32)
    for part in range(2):
        rows = slice(part * half, (part + 1) * half)
        grams += dot_split(jnp.concatenate([ab[rows], b[rows]], axis=0), ab[rows], dot_t)
    shots = dot_split(h, jnp.concatenate([b, p], axis=0), dot_t)
    pieces = [grams[:half], grams[half:]]
    for n in range(2):
        q = shots[:, n * both : (n + 1) * both]
        pieces.append(q[:half, :half] + q[half:, half:])
        pieces.append(q[:half, half:] - q[half:, :half])
    out_ref[...] = jnp.concatenate(pieces, axis=1)


def gram_two_kernel(shift, pos, b_ref, p_ref, a_ref, out_ref):
    slots, both, _ = b_ref.shape
    half = both // 2
    total = jnp.zeros((half, 3 * half), F32)
    for n in range(slots):
        s = jnp.bitwise_xor(pos[1] // 2, n)
        for part in range(2):
            rows = slice(part * half, (part + 1) * half)
            b, p, a = b_ref[s, rows], p_ref[s, rows], a_ref[s, rows]
            total += dot_split(a, jnp.concatenate([a, p + shift * b, b], axis=0), dot_t)
    out_ref[...] = total


def eliminate(m, size):
    index = lax.broadcasted_iota(jnp.int32, m.shape, 0)
    column = jnp.broadcast_to(m[:, :1], m.shape)
    for k in range(size):
        ahead = jnp.broadcast_to(m[:, k + 1 : k + 2], m.shape)
        scale = 1.0 / column[k : k + 1]
        row = m[k : k + 1] * scale
        first = ahead[k : k + 1] * scale
        m = jnp.where(index == k, row, m - column * row)
        column = jnp.where(index == k, first, ahead - column * first)
    return m


def unit_padding(size, fields):
    r = lax.broadcasted_iota(jnp.int32, (size, size), 0)
    c = lax.broadcasted_iota(jnp.int32, (size, size), 1)
    return jnp.where((r == c) & (r >= fields), 1.0, 0.0)


def invert_kernel(fields, g1_ref, out_ref):
    half = g1_ref.shape[0]
    pad = unit_padding(half, fields)
    r = lax.broadcasted_iota(jnp.int32, (half, half), 0)
    c = lax.broadcasted_iota(jnp.int32, (half, half), 1)
    eye = jnp.where(r == c, 1.0, 0.0)
    m = jnp.concatenate([g1_ref[:, :half] + pad, eye, g1_ref[:, half : 2 * half].T], axis=1)
    m = eliminate(m, fields)
    out_ref[...] = m[:, half:]


def solve_kernel(fields, pos, inv_ref, g1_ref, g2_ref, b_ref, p_ref, x_ref, c_ref):
    half = inv_ref.shape[0]
    cols, both, width = p_ref.shape
    g2 = g2_ref[0]
    for n in range(1, g2_ref.shape[0]):
        g2 = g2 + g2_ref[n]
    z22 = g2[:, :half] + unit_padding(half, fields)
    z21 = g2[:, half : 2 * half]
    z2b = g2[:, 2 * half : 3 * half]
    inv = inv_ref[:, :half]
    w1b = inv_ref[:, half:]
    mixed = dot_t(inv, z21, highest)
    step = dot_n(z21, jnp.concatenate([mixed, w1b], axis=1))
    m = eliminate(jnp.concatenate([z22, z2b], axis=1) - step, fields)
    w2 = m[:, half:]
    w1 = w1b - dot_n(mixed, w2)
    y1 = w1.T
    y2 = w2.T
    for n in range(2):
        hb = g1_ref[:, (2 + n) * half : (3 + n) * half]
        hp = g1_ref[:, (4 + n) * half : (5 + n) * half]
        total = dot_t(hb, y1, highest) + dot_t(hp, y2, highest)
        c_ref[:, n, :] = total[: c_ref.shape[0], :fields]
    y = jnp.concatenate([y1, y2], axis=1)
    for q in range(cols):
        place = jnp.bitwise_xor(pos[1], q)
        for part in range(2):
            rows = slice(part * half, (part + 1) * half)
            basis = jnp.concatenate([b_ref[place, rows], p_ref[place, rows]], axis=0)
            x = dot_split(y, basis, dot_n)
            x_ref[:, part, q * width : (q + 1) * width] = x[:fields]


def whole_call(kernel, out_shape, name, *args, scalars=0, cost=None):
    vmem = pl.BlockSpec(memory_space=pltpu.VMEM)
    smem = pl.BlockSpec(memory_space=pltpu.SMEM)
    single = not isinstance(out_shape, (list, tuple))
    return pl.pallas_call(
        kernel,
        in_specs=[smem] * scalars + [vmem] * (len(args) - scalars),
        out_specs=vmem if single else [vmem] * len(out_shape),
        out_shape=out_shape,
        cost_estimate=cost,
        compiler_params=pltpu.CompilerParams(vmem_limit_bytes=12 * MIB),
        name=name,
    )(*args)


def swap(array, axis, bit):
    size = lax.axis_size(axis)
    return lax.ppermute(array, axis, [(n, n ^ bit) for n in range(size)])


def spread(array, axis):
    size = lax.axis_size(axis)
    copies = jnp.broadcast_to(array[None], (size,) + array.shape)
    return lax.all_to_all(copies, axis, 0, 0)


def spread_start(array, axis):
    size = lax.axis_size(axis)
    return jnp.broadcast_to(array[None], (size,) + array.shape)


def body(incident, diagonal, near_blocks, left_factors, right_factors, flags, ranks, harmonics):
    _, blocks, _, rank, elements = left_factors.shape
    slots, width = near_blocks.shape[1], near_blocks.shape[4]
    fields = incident.shape[1]
    cols, rows = lax.axis_size("col"), lax.axis_size("row")
    row_index, column = lax.axis_index("row"), lax.axis_index("col")
    half = -(-fields // 8) * 8
    cluster = column * blocks + jnp.arange(blocks, dtype=jnp.int32)
    offset = (cluster - row_index + slots // 2) % rows
    is_near = jnp.any(
        (offset[:, None] == jnp.arange(slots)[None, :]) & (flags[0][None, :] == 1), axis=1
    )
    used = jnp.where(is_near, 0, ranks[0])
    pos = jnp.concatenate([jnp.stack([row_index, column]).astype(jnp.int32), flags[0], used])
    bits = [1 << n for n in range(cols.bit_length() - 1)]
    row_bits = [1 << n for n in range(rows.bit_length() - 1)]

    def place(s):
        return jnp.bitwise_xor(column, s) * width

    def cut(array, s):
        piece = lax.dynamic_slice_in_dim(array, place(s), width, 2)
        piece = jnp.pad(piece, ((0, 0), (0, half - array.shape[1]), (0, 0)))
        return piece.reshape(2 * half, width)

    def sent(array):
        array = array.astype(BF16)
        return jnp.concatenate([array[:fields], array[half : half + fields]], axis=0)

    b_first = cut(incident, 0)
    copies = spread_start(sent(b_first), "row")
    copies, right_in = lax.optimization_barrier((copies, right_factors))
    gathered = lax.all_to_all(copies, "row", 0, 0)

    rights = whole_call(
        cut_kernel,
        jax.ShapeDtypeStruct((cols, blocks * 2 * rank, width), BF16),
        "cut",
        column[None].astype(jnp.int32),
        right_in.reshape(blocks * 2 * rank, elements),
        scalars=1,
        cost=pl.CostEstimate(flops=0, bytes_accessed=32 * MIB, transcendentals=0),
    ).reshape(cols, blocks, 2 * rank, width)
    rights = [rights[0]] + [swap(rights[s], "col", s) for s in range(1, cols)]
    rights, gathered = lax.optimization_barrier((rights, gathered))
    lefts = left_factors.reshape(1, blocks * 2 * rank, elements)
    right_all = jnp.stack(rights)

    def operator(gathered, one=None):
        t = whole_call(
            functools.partial(far_in_kernel, blocks),
            jax.ShapeDtypeStruct((cols, blocks, half, 2 * rank), F32),
            "far_in",
            pos,
            gathered,
            right_all,
            scalars=1,
        )
        t = functools.reduce(jnp.add, [t[0]] + [swap(t[s], "col", s) for s in range(1, cols)])
        total = near(pos, gathered, near_blocks, 2 * half)
        if one is not None:
            total, one = lax.optimization_barrier((total, one + swap(one, "row", row_bits[-1])))
        total = whole_call(
            far_out_kernel,
            jax.ShapeDtypeStruct((cols, 2 * half, width), F32),
            "far_out",
            pos,
            t[None],
            lefts,
            total,
            scalars=1,
        )
        return total if one is None else (total, one)

    total = operator(gathered)
    total = total[0::2] + swap(total[1::2], "col", 1)
    for bit in reversed(bits[1:]):
        n = total.shape[0] // 2
        total = total[:n] + swap(total[n:], "col", bit)
    d_first = lax.dynamic_slice_in_dim(diagonal, place(0), width, 0)
    p_first = total[0] + (d_first - SHIFT)[None, :] * b_first

    copies = spread_start(sent(p_first), "row")
    copies, p_early = lax.optimization_barrier((copies, p_first))
    gathered = lax.all_to_all(copies, "row", 0, 0)

    one = whole_call(
        functools.partial(gram_one_kernel, SHIFT),
        jax.ShapeDtypeStruct((half, 6 * half), F32),
        "gram_one",
        b_first,
        p_early,
        cut(harmonics, 0),
    )
    for bit in bits:
        one = one + swap(one, "col", bit)
    b_all = jnp.stack([b_first] + [cut(incident, s) for s in range(1, cols)])
    b_own = b_all[0::2]
    p_own = p_early[None]
    for bit in bits[1:]:
        p_own = jnp.concatenate([p_own, swap(p_own, "col", bit)])
    gathered, one, p_own = lax.optimization_barrier((gathered, one, p_own))
    p_all = jnp.stack([p_own, swap(p_own, "col", 1)], axis=1).reshape(cols, 2 * half, width)

    total, one = operator(gathered, one)
    for bit in reversed(row_bits[1:-1]):
        one = one + swap(one, "row", bit)
    total = (total[0::2] + swap(total[1::2], "col", 1)).astype(BF16)
    for bit in bits[1:]:
        other = swap(total, "col", bit).astype(F32)
        total = total.astype(F32) + jnp.stack([other[s ^ (bit // 2)] for s in range(cols // 2)])
        total = total if bit == bits[-1] else total.astype(BF16)
    d_own = jnp.stack(
        [lax.dynamic_slice_in_dim(diagonal, place(s), width, 0) for s in range(0, cols, 2)]
    )
    ap, one = lax.optimization_barrier((total + d_own[:, None, :] * p_own, one))
    one = one + swap(one, "row", row_bits[0])
    two = whole_call(
        functools.partial(gram_two_kernel, SHIFT),
        jax.ShapeDtypeStruct((half, 3 * half), F32),
        "gram_two",
        pos,
        b_own,
        p_own,
        ap,
        scalars=1,
    )
    two = spread(two + swap(two, "col", 1), "row")
    inverse = whole_call(
        functools.partial(invert_kernel, fields),
        jax.ShapeDtypeStruct((half, 2 * half), F32),
        "invert",
        one,
    )
    return tuple(
        array.transpose(1, 0, 2)
        for array in whole_call(
            functools.partial(solve_kernel, fields),
            [
                jax.ShapeDtypeStruct((fields, 2, elements), F32),
                jax.ShapeDtypeStruct((harmonics.shape[1], 2, fields), F32),
            ],
            "solve",
            pos,
            inverse,
            one,
            two,
            b_all,
            p_all,
            scalars=1,
        )
    )


def solution(mesh):
    in_specs = (
        P(None, None, "row"),
        P("row"),
        P("row", None, None, None, "col"),
        P("row", "col", None, None, None),
        P("row", "col", None, None, None),
        P("row", None),
        P("row", "col"),
        P(None, None, "row"),
    )
    out_specs = (P(None, None, "row"), P())
    return jax.shard_map(body, mesh=mesh, in_specs=in_specs, out_specs=out_specs, check_vma=False)
```

```python
import functools

import jax
import jax.numpy as jnp
from jax import lax
from jax.experimental import pallas as pl
from jax.experimental.pallas import tpu as pltpu
from jax.sharding import PartitionSpec as P

F32 = jnp.float32
BF16 = jnp.bfloat16
SHIFT = 1.5
highest = lax.Precision.HIGHEST
MIB = 1024 * 1024


def dot_t(left, right, precision=None):
    return lax.dot_general(
        left, right, (((1,), (1,)), ((), ())), precision=precision, preferred_element_type=F32
    )


def dot_n(left, right, precision=highest):
    return lax.dot_general(
        left, right, (((1,), (0,)), ((), ())), precision=precision, preferred_element_type=F32
    )


def split(a):
    high = a.astype(BF16)
    return high, (a - high.astype(F32)).astype(BF16)


def dot_split(left, right, dot):
    (lh, ll), (rh, rl) = split(left), split(right)
    return dot(lh, rh, None) + (dot(lh, rl, None) + dot(ll, rh, None))


def near_kernel(rows, flags, v_ref, blocks_ref, out_ref, held, first, second, sems):
    slots = held.shape[0]
    half = out_ref.shape[0] // 2

    def fetch(k, part):
        return pltpu.make_async_copy(
            blocks_ref.at[0, k, part], held.at[k, part], sems.at[k, part]
        )

    for k in range(slots):
        for part in range(2):
            fetch(k, part).start()
    for k in range(slots):
        v = v_ref[(lax.axis_index("row") + k - slots // 2 + rows) % rows]
        v = jnp.where(flags[:, k : k + 1] == 1, v.astype(F32), 0.0).astype(BF16)
        for part in range(2):
            fetch(k, part).wait()
        for part, total in enumerate((first, second)):
            term = dot_t(v, held[k, part])
            if k == 0:
                total[...] = term
            else:
                total[...] += term
    fields = v_ref.shape[1] // 2
    out_ref[...] = jnp.zeros_like(out_ref)
    out_ref[:fields] = first[:fields] - second[fields:]
    out_ref[half : half + fields] = first[fields:] + second[:fields]


def near(flags, v, blocks, both):
    rows, twice, _ = v.shape
    _, slots, _, elements, width = blocks.shape
    return pl.pallas_call(
        functools.partial(near_kernel, rows),
        in_specs=[
            pl.BlockSpec(memory_space=pltpu.VMEM),
            pl.BlockSpec(memory_space=pltpu.VMEM),
            pl.BlockSpec(memory_space=pltpu.HBM),
        ],
        out_specs=pl.BlockSpec(memory_space=pltpu.VMEM),
        out_shape=jax.ShapeDtypeStruct((both, elements), F32),
        scratch_shapes=[
            pltpu.VMEM((slots, 2, elements, width), BF16),
            pltpu.VMEM((twice, elements), F32),
            pltpu.VMEM((twice, elements), F32),
            pltpu.SemaphoreType.DMA((slots, 2)),
        ],
        compiler_params=pltpu.CompilerParams(vmem_limit_bytes=53 * MIB),
        name="near",
    )(flags, v, blocks)


def far_kernel(rows, flags, ranks, v_ref, right_ref, left_ref, near_ref, out_ref):
    cols, both, width = out_ref.shape
    half = both // 2
    fields = v_ref.shape[2] // 2
    blocks, both_ranks, _ = right_ref.shape
    slots = flags.shape[1]
    rank = both_ranks // 2
    column = lax.axis_index("col")
    lane = lax.broadcasted_iota(jnp.int32, (half, both_ranks), 1)
    low = lane < rank

    def used(b):
        slot = (column * blocks + b - lax.axis_index("row") + slots // 2 + rows) % rows
        here = lax.broadcasted_iota(jnp.int32, (1, slots), 1) == slot
        is_near = jnp.max(jnp.where(here & (flags[...] == 1), 1, 0), axis=1, keepdims=True)
        return ranks[:, b : b + 1] * (1 - is_near)

    upper, lower = [], []
    for b in range(blocks):
        t = jnp.zeros((2 * fields, both_ranks), F32)
        for s in range(cols):
            part = pl.ds(pl.multiple_of(jnp.bitwise_xor(column, s) * width, width), width)
            t = t + dot_t(v_ref[s, b], right_ref[b, :, part])
        gap = jnp.zeros((half - fields, both_ranks), F32)
        real = jnp.concatenate([t[:fields], gap], axis=0)
        turned = jnp.concatenate([pltpu.roll(t, rank, 1)[fields:], gap], axis=0)
        z = jnp.where(low, real - turned, real + turned)
        z = jnp.where(lax.rem(lane, rank) < used(b), z, 0.0)
        upper.append(jnp.where(low, z, -z))
        lower.append(pltpu.roll(z, rank, 1))
    mixed = jnp.concatenate(
        [jnp.concatenate(upper, axis=1), jnp.concatenate(lower, axis=1)], axis=0
    ).astype(BF16)
    for q in range(cols):
        place = jnp.bitwise_xor(column, q)
        part = slice(q * width, (q + 1) * width)
        out_ref[place] = near_ref[:, part] + dot_n(mixed, left_ref[:, part], None)


def gram_one_kernel(shift, b_ref, p_ref, h_ref, out_ref):
    both = b_ref.shape[0]
    half = both // 2
    b, p, h = b_ref[...], p_ref[...], h_ref[...]
    ab = p + shift * b
    grams = jnp.zeros((2 * half, half), F32)
    for part in range(2):
        rows = slice(part * half, (part + 1) * half)
        grams += dot_split(jnp.concatenate([ab[rows], b[rows]], axis=0), ab[rows], dot_t)
    shots = dot_split(h, jnp.concatenate([b, p], axis=0), dot_t)
    pieces = [grams[:half], grams[half:]]
    for n in range(2):
        q = shots[:, n * both : (n + 1) * both]
        pieces.append(q[:half, :half] + q[half:, half:])
        pieces.append(q[:half, half:] - q[half:, :half])
    out_ref[...] = jnp.concatenate(pieces, axis=1)


def gram_two_kernel(shift, b_ref, p_ref, a_ref, out_ref):
    slots, both, _ = b_ref.shape
    half = both // 2
    total = jnp.zeros((half, 3 * half), F32)
    for n in range(slots):
        s = jnp.bitwise_xor(lax.axis_index("col") // 2, n)
        for part in range(2):
            rows = slice(part * half, (part + 1) * half)
            b, p, a = b_ref[s, rows], p_ref[s, rows], a_ref[s, rows]
            total += dot_split(a, jnp.concatenate([a, p + shift * b, b], axis=0), dot_t)
    out_ref[...] = total


def eliminate(m, size):
    index = lax.broadcasted_iota(jnp.int32, m.shape, 0)
    column = jnp.broadcast_to(m[:, :1], m.shape)
    for k in range(size):
        ahead = jnp.broadcast_to(m[:, k + 1 : k + 2], m.shape)
        scale = 1.0 / column[k : k + 1]
        row = m[k : k + 1] * scale
        first = ahead[k : k + 1] * scale
        m = jnp.where(index == k, row, m - column * row)
        column = jnp.where(index == k, first, ahead - column * first)
    return m


def unit_padding(size, fields):
    r = lax.broadcasted_iota(jnp.int32, (size, size), 0)
    c = lax.broadcasted_iota(jnp.int32, (size, size), 1)
    return jnp.where((r == c) & (r >= fields), 1.0, 0.0)


def invert_kernel(fields, g1_ref, out_ref):
    half = g1_ref.shape[0]
    pad = unit_padding(half, fields)
    r = lax.broadcasted_iota(jnp.int32, (half, half), 0)
    c = lax.broadcasted_iota(jnp.int32, (half, half), 1)
    eye = jnp.where(r == c, 1.0, 0.0)
    m = jnp.concatenate([g1_ref[:, :half] + pad, eye, g1_ref[:, half : 2 * half].T], axis=1)
    m = eliminate(m, fields)
    out_ref[...] = m[:, half:]


def solve_kernel(fields, inv_ref, g1_ref, g2_ref, b_ref, p_ref, x_ref, c_ref):
    half = inv_ref.shape[0]
    cols, both, width = p_ref.shape
    g2 = g2_ref[0]
    for n in range(1, g2_ref.shape[0]):
        g2 = g2 + g2_ref[n]
    z22 = g2[:, :half] + unit_padding(half, fields)
    z21 = g2[:, half : 2 * half]
    z2b = g2[:, 2 * half : 3 * half]
    inv = inv_ref[:, :half]
    w1b = inv_ref[:, half:]
    mixed = dot_t(inv, z21, highest)
    step = dot_n(z21, jnp.concatenate([mixed, w1b], axis=1))
    m = eliminate(jnp.concatenate([z22, z2b], axis=1) - step, fields)
    w2 = m[:, half:]
    w1 = w1b - dot_n(mixed, w2)
    y1 = w1.T
    y2 = w2.T
    for n in range(2):
        hb = g1_ref[:, (2 + n) * half : (3 + n) * half]
        hp = g1_ref[:, (4 + n) * half : (5 + n) * half]
        total = dot_t(hb, y1, highest) + dot_t(hp, y2, highest)
        c_ref[:, n, :] = total[: c_ref.shape[0], :fields]
    y = jnp.concatenate([y1, y2], axis=1)
    for q in range(cols):
        place = jnp.bitwise_xor(lax.axis_index("col"), q)
        for part in range(2):
            rows = slice(part * half, (part + 1) * half)
            basis = jnp.concatenate([b_ref[place, rows], p_ref[place, rows]], axis=0)
            x = dot_split(y, basis, dot_n)
            x_ref[:, part, q * width : (q + 1) * width] = x[:fields]


def whole_call(kernel, out_shape, name, *args, cost=None):
    vmem = pl.BlockSpec(memory_space=pltpu.VMEM)
    single = not isinstance(out_shape, (list, tuple))
    return pl.pallas_call(
        kernel,
        in_specs=[vmem] * len(args),
        out_specs=vmem if single else [vmem] * len(out_shape),
        out_shape=out_shape,
        cost_estimate=cost,
        compiler_params=pltpu.CompilerParams(vmem_limit_bytes=12 * MIB),
        name=name,
    )(*args)


def swap(array, axis, bit):
    size = lax.axis_size(axis)
    return lax.ppermute(array, axis, [(n, n ^ bit) for n in range(size)])


def spread(array, axis):
    size = lax.axis_size(axis)
    copies = jnp.broadcast_to(array[None], (size,) + array.shape)
    return lax.all_to_all(copies, axis, 0, 0)


def spread_start(array, axis):
    size = lax.axis_size(axis)
    return jnp.broadcast_to(array[None], (size,) + array.shape)


def body(incident, diagonal, near_blocks, left_factors, right_factors, flags, ranks, harmonics):
    _, blocks, _, rank, elements = left_factors.shape
    slots, width = near_blocks.shape[1], near_blocks.shape[4]
    fields = incident.shape[1]
    cols, rows = lax.axis_size("col"), lax.axis_size("row")
    column = lax.axis_index("col")
    half = -(-fields // 8) * 8
    bits = [1 << n for n in range(cols.bit_length() - 1)]
    row_bits = [1 << n for n in range(rows.bit_length() - 1)]

    def place(s):
        return jnp.bitwise_xor(column, s) * width

    def cut(array, s):
        piece = lax.dynamic_slice_in_dim(array, place(s), width, 2)
        piece = jnp.pad(piece, ((0, 0), (0, half - array.shape[1]), (0, 0)))
        return piece.reshape(2 * half, width)

    def sent(array):
        array = array.astype(BF16)
        return jnp.concatenate([array[:fields], array[half : half + fields]], axis=0)

    b_first = cut(incident, 0)
    copies = spread_start(sent(b_first), "row")
    gathered = lax.all_to_all(copies, "row", 0, 0)
    rights = right_factors.reshape(blocks, 2 * rank, elements)
    lefts = left_factors.reshape(blocks * 2 * rank, elements)

    def operator(gathered, one=None):
        def piece(s):
            return lax.dynamic_slice_in_dim(
                gathered, jnp.bitwise_xor(column, s) * blocks, blocks, 0
            )

        pieces = [piece(0)] + [swap(piece(s), "col", s) for s in range(1, cols)]
        total = near(flags, gathered, near_blocks, 2 * half)
        if one is not None:
            total, one = lax.optimization_barrier((total, one + swap(one, "row", row_bits[-1])))
        total = whole_call(
            functools.partial(far_kernel, rows),
            jax.ShapeDtypeStruct((cols, 2 * half, width), F32),
            "far",
            flags,
            ranks,
            jnp.stack(pieces),
            rights,
            lefts,
            total,
        )
        return total if one is None else (total, one)

    total = operator(gathered)
    total = total[0::2] + swap(total[1::2], "col", 1)
    for bit in reversed(bits[1:]):
        n = total.shape[0] // 2
        total = total[:n] + swap(total[n:], "col", bit)
    d_first = lax.dynamic_slice_in_dim(diagonal, place(0), width, 0)
    p_first = total[0] + (d_first - SHIFT)[None, :] * b_first

    copies = spread_start(sent(p_first), "row")
    copies, p_early = lax.optimization_barrier((copies, p_first))
    gathered = lax.all_to_all(copies, "row", 0, 0)

    one = whole_call(
        functools.partial(gram_one_kernel, SHIFT),
        jax.ShapeDtypeStruct((half, 6 * half), F32),
        "gram_one",
        b_first,
        p_early,
        cut(harmonics, 0),
    )
    for bit in bits:
        one = one + swap(one, "col", bit)
    b_all = jnp.stack([b_first] + [cut(incident, s) for s in range(1, cols)])
    b_own = b_all[0::2]
    p_own = p_early[None]
    for bit in bits[1:]:
        p_own = jnp.concatenate([p_own, swap(p_own, "col", bit)])
    gathered, one, p_own = lax.optimization_barrier((gathered, one, p_own))
    p_all = jnp.stack([p_own, swap(p_own, "col", 1)], axis=1).reshape(cols, 2 * half, width)

    total, one = operator(gathered, one)
    for bit in reversed(row_bits[1:-1]):
        one = one + swap(one, "row", bit)
    total = (total[0::2] + swap(total[1::2], "col", 1)).astype(BF16)
    for bit in bits[1:]:
        other = swap(total, "col", bit).astype(F32)
        total = total.astype(F32) + jnp.stack([other[s ^ (bit // 2)] for s in range(cols // 2)])
        total = total if bit == bits[-1] else total.astype(BF16)
    d_own = jnp.stack(
        [lax.dynamic_slice_in_dim(diagonal, place(s), width, 0) for s in range(0, cols, 2)]
    )
    ap, one = lax.optimization_barrier((total + d_own[:, None, :] * p_own, one))
    one = one + swap(one, "row", row_bits[0])
    two = whole_call(
        functools.partial(gram_two_kernel, SHIFT),
        jax.ShapeDtypeStruct((half, 3 * half), F32),
        "gram_two",
        b_own,
        p_own,
        ap,
    )
    two = spread(two + swap(two, "col", 1), "row")
    inverse = whole_call(
        functools.partial(invert_kernel, fields),
        jax.ShapeDtypeStruct((half, 2 * half), F32),
        "invert",
        one,
    )
    return tuple(
        array.transpose(1, 0, 2)
        for array in whole_call(
            functools.partial(solve_kernel, fields),
            [
                jax.ShapeDtypeStruct((fields, 2, elements), F32),
                jax.ShapeDtypeStruct((harmonics.shape[1], 2, fields), F32),
            ],
            "solve",
            inverse,
            one,
            two,
            b_all,
            p_all,
        )
    )


def solution(mesh):
    in_specs = (
        P(None, None, "row"),
        P("row"),
        P("row", None, None, None, "col"),
        P("row", "col", None, None, None),
        P("row", "col", None, None, None),
        P("row", None),
        P("row", "col"),
        P(None, None, "row"),
    )
    out_specs = (P(None, None, "row"), P())
    return jax.shard_map(body, mesh=mesh, in_specs=in_specs, out_specs=out_specs, check_vma=False)
```

```python
import functools

import jax
import jax.numpy as jnp
from jax import lax
from jax.experimental import pallas as pl
from jax.experimental.pallas import tpu as pltpu
from jax.sharding import PartitionSpec as P

F32 = jnp.float32
BF16 = jnp.bfloat16
SHIFT = 1.5
highest = lax.Precision.HIGHEST
MIB = 1024 * 1024


def dot_t(left, right, precision=None):
    return lax.dot_general(
        left, right, (((1,), (1,)), ((), ())), precision=precision, preferred_element_type=F32
    )


def dot_n(left, right, precision=highest):
    return lax.dot_general(
        left, right, (((1,), (0,)), ((), ())), precision=precision, preferred_element_type=F32
    )


def split(a):
    high = a.astype(BF16)
    return high, (a - high.astype(F32)).astype(BF16)


def dot_split(left, right, dot):
    (lh, ll), (rh, rl) = split(left), split(right)
    return dot(lh, rh, None) + (dot(lh, rl, None) + dot(ll, rh, None))


def near_kernel(rows, flags, v_ref, blocks_ref, out_ref, held, first, second, sems):
    slots = held.shape[0]
    half = out_ref.shape[0] // 2

    def fetch(k, part):
        return pltpu.make_async_copy(
            blocks_ref.at[0, k, part], held.at[k, part], sems.at[k, part]
        )

    for k in range(slots):
        for part in range(2):
            fetch(k, part).start()
    for k in range(slots):
        v = v_ref[(lax.axis_index("row") + k - slots // 2 + rows) % rows]
        v = jnp.where(flags[:, k : k + 1] > 0.5, v.astype(F32), 0.0).astype(BF16)
        for part in range(2):
            fetch(k, part).wait()
        for part, total in enumerate((first, second)):
            term = dot_t(v, held[k, part])
            if k == 0:
                total[...] = term
            else:
                total[...] += term
    fields = v_ref.shape[1] // 2
    out_ref[...] = jnp.zeros_like(out_ref)
    out_ref[:fields] = first[:fields] - second[fields:]
    out_ref[half : half + fields] = first[fields:] + second[:fields]


def near(flags, v, blocks, both):
    rows, twice, _ = v.shape
    _, slots, _, elements, width = blocks.shape
    return pl.pallas_call(
        functools.partial(near_kernel, rows),
        in_specs=[
            pl.BlockSpec(memory_space=pltpu.VMEM),
            pl.BlockSpec(memory_space=pltpu.VMEM),
            pl.BlockSpec(memory_space=pltpu.HBM),
        ],
        out_specs=pl.BlockSpec(memory_space=pltpu.VMEM),
        out_shape=jax.ShapeDtypeStruct((both, elements), F32),
        scratch_shapes=[
            pltpu.VMEM((slots, 2, elements, width), BF16),
            pltpu.VMEM((twice, elements), F32),
            pltpu.VMEM((twice, elements), F32),
            pltpu.SemaphoreType.DMA((slots, 2)),
        ],
        compiler_params=pltpu.CompilerParams(vmem_limit_bytes=53 * MIB),
        name="near",
    )(flags, v, blocks)


def far_kernel(rows, flags, ranks, v_ref, right_ref, left_ref, near_ref, out_ref):
    cols, both, width = out_ref.shape
    half = both // 2
    fields = v_ref.shape[2] // 2
    blocks, both_ranks, _ = right_ref.shape
    slots = flags.shape[1]
    rank = both_ranks // 2
    column = lax.axis_index("col")
    lane = lax.broadcasted_iota(jnp.int32, (half, both_ranks), 1)
    low = lane < rank

    def used(b):
        slot = (column * blocks + b - lax.axis_index("row") + slots // 2 + rows) % rows
        here = lax.broadcasted_iota(jnp.int32, (1, slots), 1) == slot
        is_near = jnp.max(jnp.where(here & (flags[...] == 1), 1, 0), axis=1, keepdims=True)
        return ranks[:, b : b + 1] * (1 - is_near)

    upper, lower = [], []
    for b in range(blocks):
        t = jnp.zeros((2 * fields, both_ranks), F32)
        for s in range(cols):
            part = pl.ds(pl.multiple_of(jnp.bitwise_xor(column, s) * width, width), width)
            t = t + dot_t(v_ref[s, b], right_ref[b, :, part])
        gap = jnp.zeros((half - fields, both_ranks), F32)
        real = jnp.concatenate([t[:fields], gap], axis=0)
        turned = jnp.concatenate([pltpu.roll(t, rank, 1)[fields:], gap], axis=0)
        z = jnp.where(low, real - turned, real + turned)
        z = jnp.where(lax.rem(lane, rank) < used(b), z, 0.0)
        upper.append(jnp.where(low, z, -z))
        lower.append(pltpu.roll(z, rank, 1))
    mixed = jnp.concatenate(
        [jnp.concatenate(upper, axis=1), jnp.concatenate(lower, axis=1)], axis=0
    ).astype(BF16)
    for q in range(cols):
        place = jnp.bitwise_xor(column, q)
        part = slice(q * width, (q + 1) * width)
        out_ref[place] = near_ref[:, part] + dot_n(mixed, left_ref[:, part], None)


def gram_one_kernel(shift, b_ref, p_ref, h_ref, out_ref):
    both = b_ref.shape[0]
    half = both // 2
    b, p, h = b_ref[...], p_ref[...], h_ref[...]
    ab = p + shift * b
    grams = jnp.zeros((2 * half, half), F32)
    for part in range(2):
        rows = slice(part * half, (part + 1) * half)
        grams += dot_split(jnp.concatenate([ab[rows], b[rows]], axis=0), ab[rows], dot_t)
    shots = dot_split(h, jnp.concatenate([b, p], axis=0), dot_t)
    pieces = [grams[:half], grams[half:]]
    for n in range(2):
        q = shots[:, n * both : (n + 1) * both]
        pieces.append(q[:half, :half] + q[half:, half:])
        pieces.append(q[:half, half:] - q[half:, :half])
    out_ref[...] = jnp.concatenate(pieces, axis=1)


def gram_two_kernel(shift, b_ref, p_ref, a_ref, out_ref):
    slots, both, _ = b_ref.shape
    half = both // 2
    total = jnp.zeros((half, 3 * half), F32)
    for n in range(slots):
        s = jnp.bitwise_xor(lax.axis_index("col") // 2, n)
        for part in range(2):
            rows = slice(part * half, (part + 1) * half)
            b, p, a = b_ref[s, rows], p_ref[s, rows], a_ref[s, rows]
            total += dot_split(a, jnp.concatenate([a, p + shift * b, b], axis=0), dot_t)
    out_ref[...] = total


def eliminate(m, size):
    index = lax.broadcasted_iota(jnp.int32, m.shape, 0)
    column = jnp.broadcast_to(m[:, :1], m.shape)
    for k in range(size):
        ahead = jnp.broadcast_to(m[:, k + 1 : k + 2], m.shape)
        scale = 1.0 / column[k : k + 1]
        row = m[k : k + 1] * scale
        first = ahead[k : k + 1] * scale
        m = jnp.where(index == k, row, m - column * row)
        column = jnp.where(index == k, first, ahead - column * first)
    return m


def unit_padding(size, fields):
    r = lax.broadcasted_iota(jnp.int32, (size, size), 0)
    c = lax.broadcasted_iota(jnp.int32, (size, size), 1)
    return jnp.where((r == c) & (r >= fields), 1.0, 0.0)


def invert_kernel(fields, g1_ref, out_ref):
    half = g1_ref.shape[0]
    pad = unit_padding(half, fields)
    r = lax.broadcasted_iota(jnp.int32, (half, half), 0)
    c = lax.broadcasted_iota(jnp.int32, (half, half), 1)
    eye = jnp.where(r == c, 1.0, 0.0)
    m = jnp.concatenate([g1_ref[:, :half] + pad, eye, g1_ref[:, half : 2 * half].T], axis=1)
    m = eliminate(m, fields)
    out_ref[...] = m[:, half:]


def solve_kernel(fields, inv_ref, g1_ref, g2_ref, b_ref, p_ref, x_ref, c_ref):
    half = inv_ref.shape[0]
    cols, both, width = p_ref.shape
    g2 = g2_ref[0]
    for n in range(1, g2_ref.shape[0]):
        g2 = g2 + g2_ref[n]
    z22 = g2[:, :half] + unit_padding(half, fields)
    z21 = g2[:, half : 2 * half]
    z2b = g2[:, 2 * half : 3 * half]
    inv = inv_ref[:, :half]
    w1b = inv_ref[:, half:]
    mixed = dot_t(inv, z21, highest)
    step = dot_n(z21, jnp.concatenate([mixed, w1b], axis=1))
    m = eliminate(jnp.concatenate([z22, z2b], axis=1) - step, fields)
    w2 = m[:, half:]
    w1 = w1b - dot_n(mixed, w2)
    y1 = w1.T
    y2 = w2.T
    for n in range(2):
        hb = g1_ref[:, (2 + n) * half : (3 + n) * half]
        hp = g1_ref[:, (4 + n) * half : (5 + n) * half]
        total = dot_t(hb, y1, highest) + dot_t(hp, y2, highest)
        c_ref[:, n, :] = total[: c_ref.shape[0], :fields]
    y = jnp.concatenate([y1, y2], axis=1)
    for q in range(cols):
        place = jnp.bitwise_xor(lax.axis_index("col"), q)
        for part in range(2):
            rows = slice(part * half, (part + 1) * half)
            basis = jnp.concatenate([b_ref[place, rows], p_ref[place, rows]], axis=0)
            x = dot_split(y, basis, dot_n)
            x_ref[:, part, q * width : (q + 1) * width] = x[:fields]


def whole_call(kernel, out_shape, name, *args, cost=None):
    vmem = pl.BlockSpec(memory_space=pltpu.VMEM)
    single = not isinstance(out_shape, (list, tuple))
    return pl.pallas_call(
        kernel,
        in_specs=[vmem] * len(args),
        out_specs=vmem if single else [vmem] * len(out_shape),
        out_shape=out_shape,
        cost_estimate=cost,
        compiler_params=pltpu.CompilerParams(vmem_limit_bytes=12 * MIB),
        name=name,
    )(*args)


def swap(array, axis, bit):
    size = lax.axis_size(axis)
    return lax.ppermute(array, axis, [(n, n ^ bit) for n in range(size)])


def spread(array, axis):
    size = lax.axis_size(axis)
    copies = jnp.broadcast_to(array[None], (size,) + array.shape)
    return lax.all_to_all(copies, axis, 0, 0)


def spread_start(array, axis):
    size = lax.axis_size(axis)
    return jnp.broadcast_to(array[None], (size,) + array.shape)


def body(incident, diagonal, near_blocks, left_factors, right_factors, flags, ranks, harmonics):
    _, blocks, _, rank, elements = left_factors.shape
    slots, width = near_blocks.shape[1], near_blocks.shape[4]
    fields = incident.shape[1]
    cols, rows = lax.axis_size("col"), lax.axis_size("row")
    column = lax.axis_index("col")
    half = -(-fields // 8) * 8
    bits = [1 << n for n in range(cols.bit_length() - 1)]
    row_bits = [1 << n for n in range(rows.bit_length() - 1)]

    def place(s):
        return jnp.bitwise_xor(column, s) * width

    def cut(array, s):
        piece = lax.dynamic_slice_in_dim(array, place(s), width, 2)
        piece = jnp.pad(piece, ((0, 0), (0, half - array.shape[1]), (0, 0)))
        return piece.reshape(2 * half, width)

    def sent(array):
        array = array.astype(BF16)
        return jnp.concatenate([array[:fields], array[half : half + fields]], axis=0)

    b_first = cut(incident, 0)
    copies = spread_start(sent(b_first), "row")
    copies, incident, diagonal, harmonics, flags = lax.optimization_barrier(
        (copies, incident, diagonal, harmonics, flags)
    )
    gathered = lax.all_to_all(copies, "row", 0, 0)
    used_slots = jnp.where(flags == 1, 1.0, 0.0)
    b_all = jnp.stack([b_first] + [cut(incident, s) for s in range(1, cols)])
    h_first = cut(harmonics, 0)
    d_own = jnp.stack(
        [lax.dynamic_slice_in_dim(diagonal, place(s), width, 0) for s in range(0, cols, 2)]
    )
    gathered, used_slots, b_all, h_first, d_own = lax.optimization_barrier(
        (gathered, used_slots, b_all, h_first, d_own)
    )
    rights = right_factors.reshape(blocks, 2 * rank, elements)
    lefts = left_factors.reshape(blocks * 2 * rank, elements)

    def operator(gathered, one=None):
        def piece(s):
            return lax.dynamic_slice_in_dim(
                gathered, jnp.bitwise_xor(column, s) * blocks, blocks, 0
            )

        pieces = [piece(0)] + [swap(piece(s), "col", s) for s in range(1, cols)]
        total = near(used_slots, gathered, near_blocks, 2 * half)
        if one is not None:
            total, one = lax.optimization_barrier((total, one + swap(one, "row", row_bits[-1])))
        total = whole_call(
            functools.partial(far_kernel, rows),
            jax.ShapeDtypeStruct((cols, 2 * half, width), F32),
            "far",
            flags,
            ranks,
            jnp.stack(pieces),
            rights,
            lefts,
            total,
        )
        return total if one is None else (total, one)

    total = operator(gathered)
    total = total[0::2] + swap(total[1::2], "col", 1)
    for bit in reversed(bits[1:]):
        n = total.shape[0] // 2
        total = total[:n] + swap(total[n:], "col", bit)
    p_first = total[0] + (d_own[0] - SHIFT)[None, :] * b_first

    copies = spread_start(sent(p_first), "row")
    copies, p_early = lax.optimization_barrier((copies, p_first))
    gathered = lax.all_to_all(copies, "row", 0, 0)

    one = whole_call(
        functools.partial(gram_one_kernel, SHIFT),
        jax.ShapeDtypeStruct((half, 6 * half), F32),
        "gram_one",
        b_first,
        p_early,
        h_first,
    )
    for bit in bits:
        one = one + swap(one, "col", bit)
    b_own = b_all[0::2]
    p_own = p_early[None]
    for bit in bits[1:]:
        p_own = jnp.concatenate([p_own, swap(p_own, "col", bit)])
    gathered, one, p_own = lax.optimization_barrier((gathered, one, p_own))
    p_all = jnp.stack([p_own, swap(p_own, "col", 1)], axis=1).reshape(cols, 2 * half, width)

    total, one = operator(gathered, one)
    for bit in reversed(row_bits[1:-1]):
        one = one + swap(one, "row", bit)
    total = (total[0::2] + swap(total[1::2], "col", 1)).astype(BF16)
    for bit in bits[1:]:
        other = swap(total, "col", bit).astype(F32)
        total = total.astype(F32) + jnp.stack([other[s ^ (bit // 2)] for s in range(cols // 2)])
        total = total if bit == bits[-1] else total.astype(BF16)
    ap = total + d_own[:, None, :] * p_own
    two = whole_call(
        functools.partial(gram_two_kernel, SHIFT),
        jax.ShapeDtypeStruct((half, 3 * half), F32),
        "gram_two",
        b_own,
        p_own,
        ap,
    )
    two, one = lax.optimization_barrier((two + swap(two, "col", 1), one))
    one = one + swap(one, "row", row_bits[0])
    two = spread(two, "row")
    inverse = whole_call(
        functools.partial(invert_kernel, fields),
        jax.ShapeDtypeStruct((half, 2 * half), F32),
        "invert",
        one,
    )
    return tuple(
        array.transpose(1, 0, 2)
        for array in whole_call(
            functools.partial(solve_kernel, fields),
            [
                jax.ShapeDtypeStruct((fields, 2, elements), F32),
                jax.ShapeDtypeStruct((harmonics.shape[1], 2, fields), F32),
            ],
            "solve",
            inverse,
            one,
            two,
            b_all,
            p_all,
        )
    )


def solution(mesh):
    in_specs = (
        P(None, None, "row"),
        P("row"),
        P("row", None, None, None, "col"),
        P("row", "col", None, None, None),
        P("row", "col", None, None, None),
        P("row", None),
        P("row", "col"),
        P(None, None, "row"),
    )
    out_specs = (P(None, None, "row"), P())
    return jax.shard_map(body, mesh=mesh, in_specs=in_specs, out_specs=out_specs, check_vma=False)
```

```python
import functools

import jax
import jax.numpy as jnp
from jax import lax
from jax.experimental import pallas as pl
from jax.experimental.pallas import tpu as pltpu
from jax.sharding import PartitionSpec as P

F32 = jnp.float32
BF16 = jnp.bfloat16
SHIFT = 1.5
highest = lax.Precision.HIGHEST
MIB = 1024 * 1024


def dot_t(left, right, precision=None):
    return lax.dot_general(
        left, right, (((1,), (1,)), ((), ())), precision=precision, preferred_element_type=F32
    )


def dot_n(left, right, precision=highest):
    return lax.dot_general(
        left, right, (((1,), (0,)), ((), ())), precision=precision, preferred_element_type=F32
    )


def split(a):
    high = a.astype(BF16)
    return high, (a - high.astype(F32)).astype(BF16)


def dot_split(left, right, dot):
    (lh, ll), (rh, rl) = split(left), split(right)
    return dot(lh, rh, None) + (dot(lh, rl, None) + dot(ll, rh, None))


def near_kernel(rows, flags, v_ref, blocks_ref, out_ref, held, first, second, sems):
    slots = held.shape[0]
    half = out_ref.shape[0] // 2

    def fetch(k, part):
        return pltpu.make_async_copy(
            blocks_ref.at[0, k, part], held.at[k, part], sems.at[k, part]
        )

    for k in range(slots):
        for part in range(2):
            fetch(k, part).start()
    for k in range(slots):
        v = v_ref[(lax.axis_index("row") + k - slots // 2 + rows) % rows]
        v = jnp.where(flags[:, k : k + 1] > 0.5, v.astype(F32), 0.0).astype(BF16)
        for part in range(2):
            fetch(k, part).wait()
        for part, total in enumerate((first, second)):
            term = dot_t(v, held[k, part])
            if k == 0:
                total[...] = term
            else:
                total[...] += term
    fields = v_ref.shape[1] // 2
    out_ref[...] = jnp.zeros_like(out_ref)
    out_ref[:fields] = first[:fields] - second[fields:]
    out_ref[half : half + fields] = first[fields:] + second[:fields]


def near(flags, v, blocks, both):
    rows, twice, _ = v.shape
    _, slots, _, elements, width = blocks.shape
    return pl.pallas_call(
        functools.partial(near_kernel, rows),
        in_specs=[
            pl.BlockSpec(memory_space=pltpu.VMEM),
            pl.BlockSpec(memory_space=pltpu.VMEM),
            pl.BlockSpec(memory_space=pltpu.HBM),
        ],
        out_specs=pl.BlockSpec(memory_space=pltpu.VMEM),
        out_shape=jax.ShapeDtypeStruct((both, elements), F32),
        scratch_shapes=[
            pltpu.VMEM((slots, 2, elements, width), BF16),
            pltpu.VMEM((twice, elements), F32),
            pltpu.VMEM((twice, elements), F32),
            pltpu.SemaphoreType.DMA((slots, 2)),
        ],
        compiler_params=pltpu.CompilerParams(vmem_limit_bytes=53 * MIB),
        name="near",
    )(flags, v, blocks)


def far_kernel(rows, flags, ranks, right_ref, left_ref, near_ref, *rest):
    *pieces, out_ref = rest
    cols, both, width = out_ref.shape
    half = both // 2
    fields = pieces[0].shape[1] // 2
    blocks, both_ranks, _ = right_ref.shape
    slots = flags.shape[1]
    rank = both_ranks // 2
    column = lax.axis_index("col")
    lane = lax.broadcasted_iota(jnp.int32, (half, both_ranks), 1)
    low = lane < rank

    def used(b):
        slot = (column * blocks + b - lax.axis_index("row") + slots // 2 + rows) % rows
        here = lax.broadcasted_iota(jnp.int32, (1, slots), 1) == slot
        is_near = jnp.max(jnp.where(here & (flags[...] == 1), 1, 0), axis=1, keepdims=True)
        return ranks[:, b : b + 1] * (1 - is_near)

    upper, lower = [], []
    for b in range(blocks):
        t = jnp.zeros((2 * fields, both_ranks), F32)
        for s in range(cols):
            part = pl.ds(pl.multiple_of(jnp.bitwise_xor(column, s) * width, width), width)
            t = t + dot_t(pieces[s][b], right_ref[b, :, part])
        gap = jnp.zeros((half - fields, both_ranks), F32)
        real = jnp.concatenate([t[:fields], gap], axis=0)
        turned = jnp.concatenate([pltpu.roll(t, rank, 1)[fields:], gap], axis=0)
        z = jnp.where(low, real - turned, real + turned)
        z = jnp.where(lax.rem(lane, rank) < used(b), z, 0.0)
        upper.append(jnp.where(low, z, -z))
        lower.append(pltpu.roll(z, rank, 1))
    mixed = jnp.concatenate(
        [jnp.concatenate(upper, axis=1), jnp.concatenate(lower, axis=1)], axis=0
    ).astype(BF16)
    for q in range(cols):
        place = jnp.bitwise_xor(column, q)
        part = slice(q * width, (q + 1) * width)
        out_ref[place] = near_ref[:, part] + dot_n(mixed, left_ref[:, part], None)


def gram_one_kernel(shift, b_ref, p_ref, h_ref, out_ref):
    both = b_ref.shape[0]
    half = both // 2
    b, p, h = b_ref[...], p_ref[...], h_ref[...]
    ab = p + shift * b
    grams = jnp.zeros((2 * half, half), F32)
    for part in range(2):
        rows = slice(part * half, (part + 1) * half)
        grams += dot_split(jnp.concatenate([ab[rows], b[rows]], axis=0), ab[rows], dot_t)
    shots = dot_split(h, jnp.concatenate([b, p], axis=0), dot_t)
    pieces = [grams[:half], grams[half:]]
    for n in range(2):
        q = shots[:, n * both : (n + 1) * both]
        pieces.append(q[:half, :half] + q[half:, half:])
        pieces.append(q[:half, half:] - q[half:, :half])
    out_ref[...] = jnp.concatenate(pieces, axis=1)


def gram_two_kernel(shift, b_ref, p_ref, a_ref, out_ref):
    slots, both, _ = b_ref.shape
    half = both // 2
    total = jnp.zeros((half, 3 * half), F32)
    for n in range(slots):
        s = jnp.bitwise_xor(lax.axis_index("col") // 2, n)
        for part in range(2):
            rows = slice(part * half, (part + 1) * half)
            b, p, a = b_ref[s, rows], p_ref[s, rows], a_ref[s, rows]
            total += dot_split(a, jnp.concatenate([a, p + shift * b, b], axis=0), dot_t)
    out_ref[...] = total


def eliminate(m, size):
    index = lax.broadcasted_iota(jnp.int32, m.shape, 0)
    column = jnp.broadcast_to(m[:, :1], m.shape)
    for k in range(size):
        ahead = jnp.broadcast_to(m[:, k + 1 : k + 2], m.shape)
        scale = 1.0 / column[k : k + 1]
        row = m[k : k + 1] * scale
        first = ahead[k : k + 1] * scale
        m = jnp.where(index == k, row, m - column * row)
        column = jnp.where(index == k, first, ahead - column * first)
    return m


def unit_padding(size, fields):
    r = lax.broadcasted_iota(jnp.int32, (size, size), 0)
    c = lax.broadcasted_iota(jnp.int32, (size, size), 1)
    return jnp.where((r == c) & (r >= fields), 1.0, 0.0)


def invert_kernel(fields, g1_ref, out_ref):
    half = g1_ref.shape[0]
    pad = unit_padding(half, fields)
    r = lax.broadcasted_iota(jnp.int32, (half, half), 0)
    c = lax.broadcasted_iota(jnp.int32, (half, half), 1)
    eye = jnp.where(r == c, 1.0, 0.0)
    m = jnp.concatenate([g1_ref[:, :half] + pad, eye, g1_ref[:, half : 2 * half].T], axis=1)
    m = eliminate(m, fields)
    out_ref[...] = m[:, half:]


def solve_kernel(fields, inv_ref, g1_ref, g2_ref, b_ref, p_ref, x_ref, c_ref):
    half = inv_ref.shape[0]
    cols, both, width = p_ref.shape
    g2 = g2_ref[0]
    for n in range(1, g2_ref.shape[0]):
        g2 = g2 + g2_ref[n]
    z22 = g2[:, :half] + unit_padding(half, fields)
    z21 = g2[:, half : 2 * half]
    z2b = g2[:, 2 * half : 3 * half]
    inv = inv_ref[:, :half]
    w1b = inv_ref[:, half:]
    mixed = dot_t(inv, z21, highest)
    step = dot_n(z21, jnp.concatenate([mixed, w1b], axis=1))
    m = eliminate(jnp.concatenate([z22, z2b], axis=1) - step, fields)
    w2 = m[:, half:]
    w1 = w1b - dot_n(mixed, w2)
    y1 = w1.T
    y2 = w2.T
    for n in range(2):
        hb = g1_ref[:, (2 + n) * half : (3 + n) * half]
        hp = g1_ref[:, (4 + n) * half : (5 + n) * half]
        total = dot_t(hb, y1, highest) + dot_t(hp, y2, highest)
        c_ref[:, n, :] = total[: c_ref.shape[0], :fields]
    y = jnp.concatenate([y1, y2], axis=1)
    for q in range(cols):
        place = jnp.bitwise_xor(lax.axis_index("col"), q)
        for part in range(2):
            rows = slice(part * half, (part + 1) * half)
            basis = jnp.concatenate([b_ref[place, rows], p_ref[place, rows]], axis=0)
            x = dot_split(y, basis, dot_n)
            x_ref[:, part, q * width : (q + 1) * width] = x[:fields]


def whole_call(kernel, out_shape, name, *args, cost=None):
    vmem = pl.BlockSpec(memory_space=pltpu.VMEM)
    single = not isinstance(out_shape, (list, tuple))
    return pl.pallas_call(
        kernel,
        in_specs=[vmem] * len(args),
        out_specs=vmem if single else [vmem] * len(out_shape),
        out_shape=out_shape,
        cost_estimate=cost,
        compiler_params=pltpu.CompilerParams(vmem_limit_bytes=12 * MIB),
        name=name,
    )(*args)


def swap(array, axis, bit):
    size = lax.axis_size(axis)
    return lax.ppermute(array, axis, [(n, n ^ bit) for n in range(size)])


def spread(array, axis):
    size = lax.axis_size(axis)
    copies = jnp.broadcast_to(array[None], (size,) + array.shape)
    return lax.all_to_all(copies, axis, 0, 0)


def spread_start(array, axis):
    size = lax.axis_size(axis)
    return jnp.broadcast_to(array[None], (size,) + array.shape)


def body(incident, diagonal, near_blocks, left_factors, right_factors, flags, ranks, harmonics):
    _, blocks, _, rank, elements = left_factors.shape
    slots, width = near_blocks.shape[1], near_blocks.shape[4]
    fields = incident.shape[1]
    cols, rows = lax.axis_size("col"), lax.axis_size("row")
    column = lax.axis_index("col")
    half = -(-fields // 8) * 8
    bits = [1 << n for n in range(cols.bit_length() - 1)]
    row_bits = [1 << n for n in range(rows.bit_length() - 1)]

    def place(s):
        return jnp.bitwise_xor(column, s) * width

    def cut(array, s):
        piece = lax.dynamic_slice_in_dim(array, place(s), width, 2)
        piece = jnp.pad(piece, ((0, 0), (0, half - array.shape[1]), (0, 0)))
        return piece.reshape(2 * half, width)

    def sent(array):
        array = array.astype(BF16)
        return jnp.concatenate([array[:fields], array[half : half + fields]], axis=0)

    b_first = cut(incident, 0)
    copies = spread_start(sent(b_first), "row")
    copies, incident, diagonal, harmonics, flags = lax.optimization_barrier(
        (copies, incident, diagonal, harmonics, flags)
    )
    gathered = lax.all_to_all(copies, "row", 0, 0)
    used_slots = jnp.where(flags == 1, 1.0, 0.0)
    b_all = jnp.stack([b_first] + [cut(incident, s) for s in range(1, cols)])
    h_first = cut(harmonics, 0)
    d_own = jnp.stack(
        [lax.dynamic_slice_in_dim(diagonal, place(s), width, 0) for s in range(0, cols, 2)]
    )
    gathered, used_slots, b_all, h_first, d_own = lax.optimization_barrier(
        (gathered, used_slots, b_all, h_first, d_own)
    )
    rights = right_factors.reshape(blocks, 2 * rank, elements)
    lefts = left_factors.reshape(blocks * 2 * rank, elements)

    def operator(gathered, one=None):
        def piece(s):
            return lax.dynamic_slice_in_dim(
                gathered, jnp.bitwise_xor(column, s) * blocks, blocks, 0
            )

        pieces = [piece(0)] + [swap(piece(s), "col", s) for s in range(1, cols)]
        total = near(used_slots, gathered, near_blocks, 2 * half)
        if one is not None:
            total, one = lax.optimization_barrier((total, one + swap(one, "row", row_bits[-1])))
        total = whole_call(
            functools.partial(far_kernel, rows),
            jax.ShapeDtypeStruct((cols, 2 * half, width), F32),
            "far",
            flags,
            ranks,
            rights,
            lefts,
            total,
            *pieces,
        )
        return total if one is None else (total, one)

    total = operator(gathered)
    total = total[0::2] + swap(total[1::2], "col", 1)
    for bit in reversed(bits[1:]):
        n = total.shape[0] // 2
        total = total[:n] + swap(total[n:], "col", bit)
    p_first = total[0] + (d_own[0] - SHIFT)[None, :] * b_first

    copies = spread_start(sent(p_first), "row")
    copies, p_early = lax.optimization_barrier((copies, p_first))
    gathered = lax.all_to_all(copies, "row", 0, 0)

    one = whole_call(
        functools.partial(gram_one_kernel, SHIFT),
        jax.ShapeDtypeStruct((half, 6 * half), F32),
        "gram_one",
        b_first,
        p_early,
        h_first,
    )
    for bit in bits:
        one = one + swap(one, "col", bit)
    b_own = b_all[0::2]
    p_own = p_early[None]
    for bit in bits[1:]:
        p_own = jnp.concatenate([p_own, swap(p_own, "col", bit)])
    gathered, one, p_own = lax.optimization_barrier((gathered, one, p_own))
    p_all = jnp.stack([p_own, swap(p_own, "col", 1)], axis=1).reshape(cols, 2 * half, width)

    total, one = operator(gathered, one)
    for bit in reversed(row_bits[1:-1]):
        one = one + swap(one, "row", bit)
    total = (total[0::2] + swap(total[1::2].astype(BF16), "col", 1).astype(F32)).astype(BF16)
    for bit in bits[1:]:
        other = swap(total, "col", bit).astype(F32)
        total = total.astype(F32) + jnp.stack([other[s ^ (bit // 2)] for s in range(cols // 2)])
        total = total if bit == bits[-1] else total.astype(BF16)
    ap = total + d_own[:, None, :] * p_own
    two = whole_call(
        functools.partial(gram_two_kernel, SHIFT),
        jax.ShapeDtypeStruct((half, 3 * half), F32),
        "gram_two",
        b_own,
        p_own,
        ap,
    )
    two, one = lax.optimization_barrier((two + swap(two, "col", 1), one))
    one = one + swap(one, "row", row_bits[0])
    two = spread(two, "row")
    inverse = whole_call(
        functools.partial(invert_kernel, fields),
        jax.ShapeDtypeStruct((half, 2 * half), F32),
        "invert",
        one,
    )
    return tuple(
        array.transpose(1, 0, 2)
        for array in whole_call(
            functools.partial(solve_kernel, fields),
            [
                jax.ShapeDtypeStruct((fields, 2, elements), F32),
                jax.ShapeDtypeStruct((harmonics.shape[1], 2, fields), F32),
            ],
            "solve",
            inverse,
            one,
            two,
            b_all,
            p_all,
        )
    )


def solution(mesh):
    in_specs = (
        P(None, None, "row"),
        P("row"),
        P("row", None, None, None, "col"),
        P("row", "col", None, None, None),
        P("row", "col", None, None, None),
        P("row", None),
        P("row", "col"),
        P(None, None, "row"),
    )
    out_specs = (P(None, None, "row"), P())
    return jax.shard_map(body, mesh=mesh, in_specs=in_specs, out_specs=out_specs, check_vma=False)
```

```python
import functools

import jax
import jax.numpy as jnp
from jax import lax
from jax.experimental import pallas as pl
from jax.experimental.pallas import tpu as pltpu
from jax.sharding import PartitionSpec as P

F32 = jnp.float32
BF16 = jnp.bfloat16
SHIFT = 1.5
highest = lax.Precision.HIGHEST
MIB = 1024 * 1024


def dot_t(left, right, precision=None):
    return lax.dot_general(
        left, right, (((1,), (1,)), ((), ())), precision=precision, preferred_element_type=F32
    )


def dot_n(left, right, precision=highest):
    return lax.dot_general(
        left, right, (((1,), (0,)), ((), ())), precision=precision, preferred_element_type=F32
    )


def split(a):
    high = a.astype(BF16)
    return high, (a - high.astype(F32)).astype(BF16)


def dot_split(left, right, dot):
    (lh, ll), (rh, rl) = split(left), split(right)
    return dot(lh, rh, None) + (dot(lh, rl, None) + dot(ll, rh, None))


def near_kernel(rows, flags, v_ref, blocks_ref, out_ref, held, first, second, sems):
    slots = held.shape[0]
    half = out_ref.shape[0] // 2

    def fetch(k, part):
        return pltpu.make_async_copy(
            blocks_ref.at[0, k, part], held.at[k, part], sems.at[k, part]
        )

    for k in range(slots):
        for part in range(2):
            fetch(k, part).start()
    for k in range(slots):
        v = v_ref[(lax.axis_index("row") + k - slots // 2 + rows) % rows]
        v = jnp.where(flags[:, k : k + 1] > 0.5, v.astype(F32), 0.0).astype(BF16)
        for part in range(2):
            fetch(k, part).wait()
        for part, total in enumerate((first, second)):
            term = dot_t(v, held[k, part])
            if k == 0:
                total[...] = term
            else:
                total[...] += term
    fields = v_ref.shape[1] // 2
    out_ref[...] = jnp.zeros_like(out_ref)
    out_ref[:fields] = first[:fields] - second[fields:]
    out_ref[half : half + fields] = first[fields:] + second[:fields]


def near(flags, v, blocks, both):
    rows, twice, _ = v.shape
    _, slots, _, elements, width = blocks.shape
    return pl.pallas_call(
        functools.partial(near_kernel, rows),
        in_specs=[
            pl.BlockSpec(memory_space=pltpu.VMEM),
            pl.BlockSpec(memory_space=pltpu.VMEM),
            pl.BlockSpec(memory_space=pltpu.HBM),
        ],
        out_specs=pl.BlockSpec(memory_space=pltpu.VMEM),
        out_shape=jax.ShapeDtypeStruct((both, elements), F32),
        scratch_shapes=[
            pltpu.VMEM((slots, 2, elements, width), BF16),
            pltpu.VMEM((twice, elements), F32),
            pltpu.VMEM((twice, elements), F32),
            pltpu.SemaphoreType.DMA((slots, 2)),
        ],
        compiler_params=pltpu.CompilerParams(vmem_limit_bytes=53 * MIB),
        name="near",
    )(flags, v, blocks)


def far_kernel(rows, flags, ranks, v_ref, right_ref, left_ref, near_ref, out_ref):
    cols, both, width = out_ref.shape
    half = both // 2
    fields = v_ref.shape[2] // 2
    blocks, both_ranks, _ = right_ref.shape
    slots = flags.shape[1]
    rank = both_ranks // 2
    column = lax.axis_index("col")
    lane = lax.broadcasted_iota(jnp.int32, (half, both_ranks), 1)
    low = lane < rank

    def used(b):
        slot = (column * blocks + b - lax.axis_index("row") + slots // 2 + rows) % rows
        here = lax.broadcasted_iota(jnp.int32, (1, slots), 1) == slot
        is_near = jnp.max(jnp.where(here & (flags[...] == 1), 1, 0), axis=1, keepdims=True)
        return ranks[:, b : b + 1] * (1 - is_near)

    upper, lower = [], []
    for b in range(blocks):
        t = jnp.zeros((2 * fields, both_ranks), F32)
        for s in range(cols):
            part = pl.ds(pl.multiple_of(jnp.bitwise_xor(column, s) * width, width), width)
            t = t + dot_t(v_ref[s, b], right_ref[b, :, part])
        gap = jnp.zeros((half - fields, both_ranks), F32)
        real = jnp.concatenate([t[:fields], gap], axis=0)
        turned = jnp.concatenate([pltpu.roll(t, rank, 1)[fields:], gap], axis=0)
        z = jnp.where(low, real - turned, real + turned)
        z = jnp.where(lax.rem(lane, rank) < used(b), z, 0.0)
        upper.append(jnp.where(low, z, -z))
        lower.append(pltpu.roll(z, rank, 1))
    mixed = jnp.concatenate(
        [jnp.concatenate(upper, axis=1), jnp.concatenate(lower, axis=1)], axis=0
    ).astype(BF16)
    for q in range(cols):
        place = jnp.bitwise_xor(column, q)
        part = slice(q * width, (q + 1) * width)
        out_ref[place] = near_ref[:, part] + dot_n(mixed, left_ref[:, part], None)


def gram_one_kernel(shift, b_ref, p_ref, h_ref, out_ref):
    both = b_ref.shape[0]
    half = both // 2
    b, p, h = b_ref[...], p_ref[...], h_ref[...]
    ab = p + shift * b
    grams = jnp.zeros((2 * half, half), F32)
    for part in range(2):
        rows = slice(part * half, (part + 1) * half)
        grams += dot_split(jnp.concatenate([ab[rows], b[rows]], axis=0), ab[rows], dot_t)
    shots = dot_split(h, jnp.concatenate([b, p], axis=0), dot_t)
    pieces = [grams[:half], grams[half:]]
    for n in range(2):
        q = shots[:, n * both : (n + 1) * both]
        pieces.append(q[:half, :half] + q[half:, half:])
        pieces.append(q[:half, half:] - q[half:, :half])
    out_ref[...] = jnp.concatenate(pieces, axis=1)


def gram_two_kernel(shift, b_ref, p_ref, a_ref, out_ref):
    slots, both, _ = b_ref.shape
    half = both // 2
    total = jnp.zeros((half, 3 * half), F32)
    for n in range(slots):
        s = jnp.bitwise_xor(lax.axis_index("col") // 2, n)
        for part in range(2):
            rows = slice(part * half, (part + 1) * half)
            b, p, a = b_ref[s, rows], p_ref[s, rows], a_ref[s, rows]
            total += dot_split(a, jnp.concatenate([a, p + shift * b, b], axis=0), dot_t)
    out_ref[...] = total


def eliminate(m, size):
    index = lax.broadcasted_iota(jnp.int32, m.shape, 0)
    column = jnp.broadcast_to(m[:, :1], m.shape)
    for k in range(size):
        ahead = jnp.broadcast_to(m[:, k + 1 : k + 2], m.shape)
        scale = 1.0 / column[k : k + 1]
        row = m[k : k + 1] * scale
        first = ahead[k : k + 1] * scale
        m = jnp.where(index == k, row, m - column * row)
        column = jnp.where(index == k, first, ahead - column * first)
    return m


def unit_padding(size, fields):
    r = lax.broadcasted_iota(jnp.int32, (size, size), 0)
    c = lax.broadcasted_iota(jnp.int32, (size, size), 1)
    return jnp.where((r == c) & (r >= fields), 1.0, 0.0)


def invert_kernel(fields, g1_ref, out_ref):
    half = g1_ref.shape[0]
    pad = unit_padding(half, fields)
    r = lax.broadcasted_iota(jnp.int32, (half, half), 0)
    c = lax.broadcasted_iota(jnp.int32, (half, half), 1)
    eye = jnp.where(r == c, 1.0, 0.0)
    m = jnp.concatenate([g1_ref[:, :half] + pad, eye, g1_ref[:, half : 2 * half].T], axis=1)
    m = eliminate(m, fields)
    out_ref[...] = m[:, half:]


def solve_kernel(fields, inv_ref, g1_ref, g2_ref, b_ref, p_ref, x_ref, c_ref):
    half = inv_ref.shape[0]
    cols, both, width = p_ref.shape
    g2 = g2_ref[0]
    for n in range(1, g2_ref.shape[0]):
        g2 = g2 + g2_ref[n]
    z22 = g2[:, :half] + unit_padding(half, fields)
    z21 = g2[:, half : 2 * half]
    z2b = g2[:, 2 * half : 3 * half]
    inv = inv_ref[:, :half]
    w1b = inv_ref[:, half:]
    mixed = dot_t(inv, z21, highest)
    step = dot_n(z21, jnp.concatenate([mixed, w1b], axis=1))
    m = eliminate(jnp.concatenate([z22, z2b], axis=1) - step, fields)
    w2 = m[:, half:]
    w1 = w1b - dot_n(mixed, w2)
    y1 = w1.T
    y2 = w2.T
    for n in range(2):
        hb = g1_ref[:, (2 + n) * half : (3 + n) * half]
        hp = g1_ref[:, (4 + n) * half : (5 + n) * half]
        total = dot_t(hb, y1, highest) + dot_t(hp, y2, highest)
        c_ref[:, n, :] = total[: c_ref.shape[0], :fields]
    y = jnp.concatenate([y1, y2], axis=1)
    for q in range(cols):
        place = jnp.bitwise_xor(lax.axis_index("col"), q)
        for part in range(2):
            rows = slice(part * half, (part + 1) * half)
            basis = jnp.concatenate([b_ref[place, rows], p_ref[place, rows]], axis=0)
            x = dot_split(y, basis, dot_n)
            x_ref[:, part, q * width : (q + 1) * width] = x[:fields]


def whole_call(kernel, out_shape, name, *args, cost=None):
    vmem = pl.BlockSpec(memory_space=pltpu.VMEM)
    single = not isinstance(out_shape, (list, tuple))
    return pl.pallas_call(
        kernel,
        in_specs=[vmem] * len(args),
        out_specs=vmem if single else [vmem] * len(out_shape),
        out_shape=out_shape,
        cost_estimate=cost,
        compiler_params=pltpu.CompilerParams(vmem_limit_bytes=12 * MIB),
        name=name,
    )(*args)


def swap(array, axis, bit):
    size = lax.axis_size(axis)
    return lax.ppermute(array, axis, [(n, n ^ bit) for n in range(size)])


def spread(array, axis):
    size = lax.axis_size(axis)
    copies = jnp.broadcast_to(array[None], (size,) + array.shape)
    return lax.all_to_all(copies, axis, 0, 0)


def spread_start(array, axis):
    size = lax.axis_size(axis)
    return jnp.broadcast_to(array[None], (size,) + array.shape)


def body(incident, diagonal, near_blocks, left_factors, right_factors, flags, ranks, harmonics):
    _, blocks, _, rank, elements = left_factors.shape
    slots, width = near_blocks.shape[1], near_blocks.shape[4]
    fields = incident.shape[1]
    cols, rows = lax.axis_size("col"), lax.axis_size("row")
    column = lax.axis_index("col")
    half = -(-fields // 8) * 8
    bits = [1 << n for n in range(cols.bit_length() - 1)]
    row_bits = [1 << n for n in range(rows.bit_length() - 1)]

    def place(s):
        return jnp.bitwise_xor(column, s) * width

    def cut(array, s):
        piece = lax.dynamic_slice_in_dim(array, place(s), width, 2)
        piece = jnp.pad(piece, ((0, 0), (0, half - array.shape[1]), (0, 0)))
        return piece.reshape(2 * half, width)

    def sent(array):
        array = array.astype(BF16)
        return jnp.concatenate([array[:fields], array[half : half + fields]], axis=0)

    b_first = cut(incident, 0)
    copies = spread_start(sent(b_first), "row")
    copies, incident, diagonal, harmonics, flags = lax.optimization_barrier(
        (copies, incident, diagonal, harmonics, flags)
    )
    gathered = lax.all_to_all(copies, "row", 0, 0)
    used_slots = jnp.where(flags == 1, 1.0, 0.0)
    b_all = jnp.stack([b_first] + [cut(incident, s) for s in range(1, cols)])
    h_first = cut(harmonics, 0)
    d_own = jnp.stack(
        [lax.dynamic_slice_in_dim(diagonal, place(s), width, 0) for s in range(0, cols, 2)]
    )
    gathered, used_slots, b_all, h_first, d_own = lax.optimization_barrier(
        (gathered, used_slots, b_all, h_first, d_own)
    )
    rights = right_factors.reshape(blocks, 2 * rank, elements)
    lefts = left_factors.reshape(blocks * 2 * rank, elements)

    def operator(gathered, one=None):
        def piece(s):
            return lax.dynamic_slice_in_dim(
                gathered, jnp.bitwise_xor(column, s) * blocks, blocks, 0
            )

        pieces = [piece(0)] + [swap(piece(s), "col", s) for s in range(1, cols)]
        total = near(used_slots, gathered, near_blocks, 2 * half)
        total = whole_call(
            functools.partial(far_kernel, rows),
            jax.ShapeDtypeStruct((cols, 2 * half, width), F32),
            "far",
            flags,
            ranks,
            jnp.stack(pieces),
            rights,
            lefts,
            total,
        )
        if one is None:
            return total
        return lax.optimization_barrier((total, one + swap(one, "row", row_bits[-1])))

    total = operator(gathered)
    total = total[0::2] + swap(total[1::2], "col", 1)
    for bit in reversed(bits[1:]):
        n = total.shape[0] // 2
        total = total[:n] + swap(total[n:], "col", bit)
    p_first = total[0] + (d_own[0] - SHIFT)[None, :] * b_first

    copies = spread_start(sent(p_first), "row")
    copies, p_early = lax.optimization_barrier((copies, p_first))
    gathered = lax.all_to_all(copies, "row", 0, 0)

    one = whole_call(
        functools.partial(gram_one_kernel, SHIFT),
        jax.ShapeDtypeStruct((half, 6 * half), F32),
        "gram_one",
        b_first,
        p_early,
        h_first,
    )
    for bit in bits:
        one = one + swap(one, "col", bit)
    b_own = b_all[0::2]
    p_own = p_early[None]
    for bit in bits[1:]:
        p_own = jnp.concatenate([p_own, swap(p_own, "col", bit)])
    gathered, one, p_own = lax.optimization_barrier((gathered, one, p_own))
    p_all = jnp.stack([p_own, swap(p_own, "col", 1)], axis=1).reshape(cols, 2 * half, width)

    total, one = operator(gathered, one)
    for bit in reversed(row_bits[1:-1]):
        one = one + swap(one, "row", bit)
    total = (total[0::2] + swap(total[1::2], "col", 1)).astype(BF16)
    for bit in bits[1:]:
        other = swap(total, "col", bit).astype(F32)
        total = total.astype(F32) + jnp.stack([other[s ^ (bit // 2)] for s in range(cols // 2)])
        total = total if bit == bits[-1] else total.astype(BF16)
    ap = total + d_own[:, None, :] * p_own
    two = whole_call(
        functools.partial(gram_two_kernel, SHIFT),
        jax.ShapeDtypeStruct((half, 3 * half), F32),
        "gram_two",
        b_own,
        p_own,
        ap,
    )
    two, one = lax.optimization_barrier((two + swap(two, "col", 1), one))
    one = one + swap(one, "row", row_bits[0])
    two = spread(two, "row")
    inverse = whole_call(
        functools.partial(invert_kernel, fields),
        jax.ShapeDtypeStruct((half, 2 * half), F32),
        "invert",
        one,
    )
    return tuple(
        array.transpose(1, 0, 2)
        for array in whole_call(
            functools.partial(solve_kernel, fields),
            [
                jax.ShapeDtypeStruct((fields, 2, elements), F32),
                jax.ShapeDtypeStruct((harmonics.shape[1], 2, fields), F32),
            ],
            "solve",
            inverse,
            one,
            two,
            b_all,
            p_all,
        )
    )


def solution(mesh):
    in_specs = (
        P(None, None, "row"),
        P("row"),
        P("row", None, None, None, "col"),
        P("row", "col", None, None, None),
        P("row", "col", None, None, None),
        P("row", None),
        P("row", "col"),
        P(None, None, "row"),
    )
    out_specs = (P(None, None, "row"), P())
    return jax.shard_map(body, mesh=mesh, in_specs=in_specs, out_specs=out_specs, check_vma=False)
```
